32 devices in a mesh: freq: 2 (over x), sx: 4 (over y, core), sy: 4 (over z).
Axes of the slice: x: 2, y: 2, z: 4, core: 2. Of those that a mesh axis runs over, the one named last changes fastest.
Arguments:
- stiffness: bfloat16 [4, 4, 3072, 3072], P('sx', 'sy', None, 'freq'), as said below
- mass_matrix: bfloat16 [4, 4, 3072, 3072], P('sx', 'sy', None, 'freq'), as said below
- omega_table: float32 [8], replicated, may hold values from 0.5 to 6
- assignment: int32 [8], P('freq'), may hold values from 0 to 7, each once
- adjoint_load: float32 [4, 4, 8, 2, 4, 768], P('sx', 'sy', 'freq'), as said below
- forward_state: bfloat16 [4, 4, 8, 2, 4, 768], P('sx', 'sy', 'freq'), may hold values from -6 to 6
- owner_index: int32 [4, 4, 4, 768], P('sx', 'sy'), may hold values from 0 to 1727
Outputs:
- adjoint: float32 [4, 4, 8, 2, 4, 768], P('sx', 'sy', 'freq')
- gradient: float32 [4, 4, 1728], P('sx', 'sy', 'freq')
- residual_level: float32 [8], P('freq')
The draws below stay inside these ranges and needn't reach their ends.
Inputs may be any that keep to these rules, and one draw needn't show every extreme that they name: `stiffness`: each substructure's K, read as in the reference program, is symmetric. `mass_matrix`: each substructure's M, read as in the reference program, is symmetric. `adjoint_load`: the two copies of a face shared by neighbouring substructures are equal.
All inputs are finite; a program needn't handle non-finite values.
Results may differ from the reference program's by a relative error of at most 0.012.
Values may be sent and summed in bfloat16 or wider, within the bound.
A program may use at most 128 MiB of HBM per device.

```python
import math
import jax
import jax.numpy as jnp
from jax import lax

NF = 768
NB = 3072
NFREQS = 8
ITERS = 4
DE_SUB = 1728
NSUBX = 4
NSUBY = 4


def symmetric_part(key, diagonal_value, spread):
    normal_draw = jax.random.normal(key, (NSUBX, NSUBY, NB, NB), jnp.float32)
    symmetric = (normal_draw + jnp.swapaxes(normal_draw, 2, 3)) * 0.5 ** 0.5
    identity = jnp.eye(NB, dtype=jnp.float32)
    matrix = diagonal_value * identity + spread / NB ** 0.5 * symmetric
    reordered = jnp.swapaxes(matrix.reshape(NSUBX, NSUBY, NB, 4, NF), 3, 4)
    return reordered.reshape(NSUBX, NSUBY, NB, 4 * NF).astype(jnp.bfloat16)


def draw_stiffness(key, part):
    return symmetric_part(jax.random.fold_in(key, 11), 4.0, 1.0)


def draw_mass_matrix(key, part):
    return symmetric_part(jax.random.fold_in(key, 23), 1.0, 0.25)


def face_values(key, count_x, count_y, shift_x):
    out_shape = (count_x, count_y, NFREQS, 2, NF)
    base_key = jax.random.fold_in(key, 5)
    level_key = jax.random.fold_in(key, 9)
    frac_x = (jnp.arange(count_x, dtype=jnp.float32) + shift_x) / NSUBX
    growth = (3.0 ** frac_x)[:, None, None, None, None]
    levels = jnp.exp(jax.random.uniform(level_key, out_shape, jnp.float32, 0.0, math.log(10.0)))
    base_draw = jax.random.normal(base_key, out_shape, jnp.float32)
    return 0.3 * base_draw * levels * growth


def draw_adjoint_load(key, part):
    faces_x = face_values(jax.random.fold_in(key, 31), NSUBX + 1, NSUBY, 0.0)
    faces_y = face_values(jax.random.fold_in(key, 37), NSUBX, NSUBY + 1, 0.5)
    return jnp.stack([faces_x[:-1], faces_x[1:], faces_y[:, :-1], faces_y[:, 1:]], axis=4)


def touch_ends(result, own_key, low, top_value):
    longest = result.shape.index(max(result.shape))
    spots = []
    for shift in (0, 1):
        where = [jax.random.randint(jax.random.fold_in(own_key, axis), (), 0, length) for axis, length in enumerate(result.shape)]
        where[longest] = (where[longest] + shift) % result.shape[longest]
        spots.append(tuple(where))
    return result.at[spots[0]].set(low).at[spots[1]].set(top_value)


def block_scale(key, dims, pieces, low, high):
    def one(axis_at, parts):
        steps = jax.random.uniform(jax.random.fold_in(jax.random.fold_in(key, 6), axis_at), (parts,), jnp.float32, low / len(pieces), high / len(pieces))
        return jnp.repeat(jnp.exp(steps), dims[axis_at] // parts).reshape((-1,) + (1,) * (len(dims) - axis_at - 1))

    gain = one(*pieces[0])
    for cut in pieces[1:]:
        gain = gain * one(*cut)
    return gain


def noise(key, shape, width, most, split=(), held_as=jnp.bfloat16):
    entries = width * jax.random.normal(key, shape, jnp.float32)
    if split:
        entries = entries * block_scale(key, shape, split, -0.22, 0.18)
    return jnp.clip(entries, -most, most).astype(held_as)


def setup_inputs(seed: int = 0) -> dict:
    key_list = jax.random.split(jax.random.key(seed), 8)
    stiffness = draw_stiffness(jax.random.fold_in(key_list[7], 71), 0)
    mass_matrix = draw_mass_matrix(jax.random.fold_in(key_list[7], 71), 0)
    omega_table = jnp.clip(jnp.exp(jax.random.uniform(key_list[2], (NFREQS,), jnp.float32, math.log(0.5), math.log(6.0))), 0.5, 6.0)
    assignment = jax.random.permutation(key_list[3], NFREQS).astype(jnp.int32)
    adjoint_load = draw_adjoint_load(jax.random.fold_in(key_list[7], 71), 0)
    forward_state = noise(key_list[5], (NSUBX, NSUBY, NFREQS, 2, 4, NF), 1.0, 6.0, ((0, 4), (1, 4), (2, 2)))
    owner_index = touch_ends(jax.random.randint(key_list[6], (NSUBX, NSUBY, 4, NF), 0, DE_SUB), jax.random.fold_in(key_list[6], 1), 0, DE_SUB - 1).astype(jnp.int32)
    return {"stiffness": stiffness, "mass_matrix": mass_matrix, "omega_table": omega_table, "assignment": assignment, "adjoint_load": adjoint_load, "forward_state": forward_state, "owner_index": owner_index}


LOSS_FACTOR = 0.3


def face_weights():
    index_x = jnp.arange(NSUBX, dtype=jnp.int32)[:, None] * jnp.ones((1, NSUBY), jnp.int32)
    index_y = jnp.ones((NSUBX, 1), jnp.int32) * jnp.arange(NSUBY, dtype=jnp.int32)[None, :]
    west_weight = jnp.where(index_x > 0, 0.5, 1.0)
    east_weight = jnp.where(index_x < NSUBX - 1, 0.5, 1.0)
    south_weight = jnp.where(index_y > 0, 0.5, 1.0)
    north_weight = jnp.where(index_y < NSUBY - 1, 0.5, 1.0)
    return jnp.stack([west_weight, east_weight, south_weight, north_weight], axis=-1).astype(jnp.float32)


def face_major(matrix):
    sub_count = NSUBX * NSUBY
    return jnp.swapaxes(matrix.reshape(sub_count, NB, NF, 4), 2, 3).reshape(sub_count, NB, NB)


def local_products(vector, stiffness, mass_matrix):
    sub_count = NSUBX * NSUBY
    stacked_rows = vector.astype(jnp.bfloat16).reshape(sub_count, NFREQS * 2, NB)
    stiff_flat = face_major(stiffness)
    mass_flat = face_major(mass_matrix)

    def per_substructure(packed):
        rows_in, stiff_one, mass_one = packed
        return (jnp.dot(rows_in, stiff_one, preferred_element_type=jnp.float32),
                jnp.dot(rows_in, mass_one, preferred_element_type=jnp.float32))

    stiff_part, mass_part = lax.map(per_substructure, (stacked_rows, stiff_flat, mass_flat))
    out_shape = (NSUBX, NSUBY, NFREQS, 2, 4, NF)
    return stiff_part.reshape(out_shape), mass_part.reshape(out_shape)


def assemble(local_vals):
    west_face = local_vals[:, :, :, :, 0]
    east_face = local_vals[:, :, :, :, 1]
    south_face = local_vals[:, :, :, :, 2]
    north_face = local_vals[:, :, :, :, 3]
    zero_row = jnp.zeros_like(west_face[:1])
    zero_col = jnp.zeros_like(south_face[:, :1])
    from_left = jnp.concatenate([zero_row, east_face[:-1]], axis=0)
    from_right = jnp.concatenate([west_face[1:], zero_row], axis=0)
    from_below = jnp.concatenate([zero_col, north_face[:, :-1]], axis=1)
    from_above = jnp.concatenate([south_face[:, 1:], zero_col], axis=1)
    return jnp.stack([west_face + from_left, east_face + from_right,
                      south_face + from_below, north_face + from_above], axis=4)


def operate(vector, stiffness, mass_matrix, omega_sq, sign_factor):
    stiff_part, mass_part = local_products(vector, stiffness, mass_matrix)
    factor = omega_sq[None, None, :, None, None]
    real_part = stiff_part[:, :, :, 0] - sign_factor * LOSS_FACTOR * stiff_part[:, :, :, 1] - factor * mass_part[:, :, :, 0]
    imag_part = stiff_part[:, :, :, 1] + sign_factor * LOSS_FACTOR * stiff_part[:, :, :, 0] - factor * mass_part[:, :, :, 1]
    return assemble(jnp.stack([real_part, imag_part], axis=3))


def inner(first_vec, second_vec, weights):
    return jnp.sum(first_vec * second_vec * weights[:, :, None, None, :, None], axis=(0, 1, 3, 4, 5))


def per_freq(values):
    return values[None, None, :, None, None, None]


def reference(stiffness, mass_matrix, omega_table, assignment, adjoint_load, forward_state, owner_index):
    omega_sq = omega_table[assignment]
    weights = face_weights()
    residual = adjoint_load
    solution = jnp.zeros_like(adjoint_load)
    normal_res = operate(residual, stiffness, mass_matrix, omega_sq, -1.0)
    direction = normal_res
    gamma_now = inner(normal_res, normal_res, weights)
    for iteration in range(ITERS):
        image_vec = operate(direction, stiffness, mass_matrix, omega_sq, 1.0)
        delta_now = inner(image_vec, image_vec, weights)
        step_size = gamma_now / delta_now
        solution = solution + per_freq(step_size) * direction
        if iteration + 1 < ITERS:
            residual = residual - per_freq(step_size) * image_vec
            normal_res = operate(residual, stiffness, mass_matrix, omega_sq, -1.0)
            gamma_next = inner(normal_res, normal_res, weights)
            direction = normal_res + per_freq(gamma_next / gamma_now) * direction
            gamma_now = gamma_next
    residual_level = jnp.log(gamma_now / float(NSUBX * NSUBY * 2 * NB))
    state_vec = forward_state.astype(jnp.float32)
    lambda_real = solution[:, :, :, 0]
    lambda_imag = solution[:, :, :, 1]
    state_real = state_vec[:, :, :, 0]
    state_imag = state_vec[:, :, :, 1]
    product_term = (lambda_real * state_real - lambda_imag * state_imag) - LOSS_FACTOR * (lambda_real * state_imag + lambda_imag * state_real)
    dof_total = jnp.sum(product_term, axis=2)
    grad_factor = (DE_SUB / (NFREQS * NB)) ** 0.5

    def per_substructure(packed):
        values, owners = packed
        return jax.ops.segment_sum(values.reshape(-1), owners.reshape(-1), num_segments=DE_SUB)

    gradient = lax.map(per_substructure, (dof_total.reshape(NSUBX * NSUBY, 4, NF),
                                          owner_index.reshape(NSUBX * NSUBY, 4, NF)))
    gradient = -grad_factor * gradient.reshape(NSUBX, NSUBY, DE_SUB)
    return solution, gradient, residual_level
```

```python
import functools

import jax
import jax.numpy as jnp
from jax import lax
from jax.experimental import pallas as pl
from jax.experimental.pallas import tpu as pltpu
from jax.sharding import PartitionSpec as P

ITERS = 4
DE_SUB = 1728


LOSS_FACTOR = 0.3


def padded(cells, sides, width):
    for axis, dim in sides:
        count = lax.axis_size(axis)
        ends = count - 1
        head = lax.slice_in_dim(cells, 0, width, axis=dim)
        tail = lax.slice_in_dim(cells, cells.shape[dim] - width, cells.shape[dim], axis=dim)
        cells = jnp.concatenate(
            [
                lax.ppermute(tail, axis, [(i, (i + 1) % count) for i in range(ends)]),
                cells,
                lax.ppermute(head, axis, [((i + 1) % count, i) for i in range(ends)]),
            ],
            axis=dim,
        )
    return cells


def face_weights():
    index_x = lax.axis_index("sx")
    size_x = lax.axis_size("sx")
    index_y = lax.axis_index("sy")
    size_y = lax.axis_size("sy")
    west_weight = jnp.where(index_x > 0, 0.5, 1.0)
    east_weight = jnp.where(index_x < size_x - 1, 0.5, 1.0)
    south_weight = jnp.where(index_y > 0, 0.5, 1.0)
    north_weight = jnp.where(index_y < size_y - 1, 0.5, 1.0)
    return jnp.stack([west_weight, east_weight, south_weight, north_weight]).astype(jnp.float32)


def assemble(local_vals):
    padded_x = padded(local_vals[:, :, 0:2].astype(jnp.bfloat16), (("sx", 2),), 1).astype(
        jnp.float32
    )
    padded_y = padded(local_vals[:, :, 2:4].astype(jnp.bfloat16), (("sy", 2),), 1).astype(
        jnp.float32
    )
    west_face = padded_x[:, :, 1] + padded_x[:, :, 0]
    east_face = padded_x[:, :, 2] + padded_x[:, :, 3]
    south_face = padded_y[:, :, 1] + padded_y[:, :, 0]
    north_face = padded_y[:, :, 2] + padded_y[:, :, 3]
    return jnp.stack([west_face, east_face, south_face, north_face], axis=2)


def mix_parts(stiff_part, mass_part, omega_sq, sign_factor):
    factor = omega_sq[:, None, None]
    real_part = (
        stiff_part[:, 0] - sign_factor * LOSS_FACTOR * stiff_part[:, 1] - factor * mass_part[:, 0]
    )
    imag_part = (
        stiff_part[:, 1] + sign_factor * LOSS_FACTOR * stiff_part[:, 0] - factor * mass_part[:, 1]
    )
    return jnp.stack([real_part, imag_part], axis=1)


def apply_rows(vector, stiff_cols, mass_cols, omega_every, sign_factor):
    face_count = vector.shape[2]
    matrix_order = face_count * vector.shape[3]
    rounded = vector.astype(jnp.bfloat16)
    pieces = lax.all_gather(rounded, "freq", axis=0, tiled=True)
    count = pieces.shape[0]
    flattened = pieces.reshape(-1, matrix_order)
    stiff_part = jnp.dot(flattened, stiff_cols, preferred_element_type=jnp.float32)
    mass_part = jnp.dot(flattened, mass_cols, preferred_element_type=jnp.float32)
    local_vals = mix_parts(
        stiff_part.reshape(count, 2, face_count, -1),
        mass_part.reshape(count, 2, face_count, -1),
        omega_every,
        sign_factor,
    )
    returned = lax.all_to_all(
        local_vals.astype(jnp.bfloat16), "freq", split_axis=0, concat_axis=3, tiled=True
    ).astype(local_vals.dtype)
    return assemble(returned)


def reduce_dots(factor_pairs, weights):
    partial_value = tuple(
        (
            jnp.sum(first_vec * second_vec * weights[None, None, :, None], axis=(1, 2, 3))
            for first_vec, second_vec in factor_pairs
        )
    )
    summed = lax.psum(partial_value, ("sx", "sy"))
    return summed


def per_freq(values):
    return values[:, None, None, None]


def face_columns(matrix, matrix_order, face_count):
    grouped = matrix.reshape(matrix_order, -1, face_count)
    return jnp.swapaxes(grouped, 1, 2).reshape(matrix_order, -1)


def body(stiffness, mass_matrix, omega_table, assignment, adjoint_load, forward_state, owner_index):
    n_freq = lax.axis_size("freq")
    slot_count = adjoint_load.shape[2]
    face_count = adjoint_load.shape[4]
    face_len = adjoint_load.shape[5]
    matrix_order = face_count * face_len
    stiff_cols = face_columns(stiffness[0, 0], matrix_order, face_count)
    mass_cols = face_columns(mass_matrix[0, 0], matrix_order, face_count)
    matches = assignment[:, None] == jnp.arange(omega_table.shape[0], dtype=jnp.int32)[None, :]
    slot_omega = jnp.sum(jnp.where(matches, omega_table[None, :], 0.0), axis=1)
    weights = face_weights()
    load_rows = adjoint_load[0, 0]
    omega_every = lax.all_gather(slot_omega, "freq", axis=0, tiled=True)

    def operate(vector, sign_factor):
        return apply_rows(vector, stiff_cols, mass_cols, omega_every, sign_factor)

    residual = load_rows
    solution = jnp.zeros_like(load_rows)
    normal_res = operate(residual, -1.0)
    direction = normal_res
    image_vec = operate(normal_res, 1.0)
    gamma_now, delta_now = reduce_dots(((normal_res, normal_res), (image_vec, image_vec)), weights)
    for iteration in range(ITERS):
        step_size = gamma_now / delta_now
        solution = solution + per_freq(step_size) * direction
        if iteration + 1 < ITERS:
            residual = residual - per_freq(step_size) * image_vec
            normal_res = operate(residual, -1.0)
            fresh = operate(normal_res, 1.0)
            gamma_next, fresh_norm, fresh_cross = reduce_dots(
                ((normal_res, normal_res), (fresh, fresh), (fresh, image_vec)), weights
            )
            beta_ratio = gamma_next / gamma_now
            direction = normal_res + per_freq(beta_ratio) * direction
            image_vec = fresh + per_freq(beta_ratio) * image_vec
            delta_now = (
                fresh_norm + 2.0 * beta_ratio * fresh_cross + beta_ratio * beta_ratio * delta_now
            )
            gamma_now = gamma_next
    cell_count = float(lax.axis_size("sx") * lax.axis_size("sy") * 2 * matrix_order)
    residual_level = jnp.log(gamma_now / cell_count)
    state_vec = forward_state[0, 0].astype(jnp.float32)
    lambda_real = solution[:, 0]
    lambda_imag = solution[:, 1]
    state_real = state_vec[:, 0]
    state_imag = state_vec[:, 1]
    product_term = (
        lambda_real * state_real
        - lambda_imag * state_imag
        - LOSS_FACTOR * (lambda_real * state_imag + lambda_imag * state_real)
    )
    dof_total = jnp.sum(product_term, axis=0)
    partial_grad = jax.ops.segment_sum(
        dof_total.reshape(-1), owner_index[0, 0].reshape(-1), num_segments=DE_SUB
    )
    grad_factor = (DE_SUB / (slot_count * n_freq * matrix_order)) ** 0.5
    gradient = lax.psum_scatter(
        -grad_factor * partial_grad, "freq", scatter_dimension=0, tiled=True
    )
    return (solution[None, None], gradient[None, None], residual_level)


MESH = pl.DeviceIdType.MESH


def fused_kernel(
    sizes, ld, st, om, own, stiff, mass, out_sol, out_grad, out_lvl,
    stage, mats, acc, vown, vpart, fsend, frecv, state, yloc, dacc, scal, hist,
    red_y, red_x, red_f, ldr, stb, stw, omr, omw, solr, gsend, grecv,
    mat_sem, pro_send, pro_recv, vs_sem, vr_sem, fs_sem, fr_sem,
    ys_sem, yr_sem, xs_sem, xr_sem, ps_sem, pr_sem, epi_send, epi_recv,
):
    n_x, n_y, face_len, cells, grad_factor = sizes
    seg = face_len // 2
    half = 2 * seg
    blocks = seg // 128
    f = lax.axis_index("freq")
    ix = lax.axis_index("sx")
    iy = lax.axis_index("sy")
    other = 1 - f
    N, PD, Q, W, FR, SOL = range(6)

    def mat_copy(m, r):
        src = stiff if m == 0 else mass
        off = (r % 4) * face_len + ((f + r // 4) % 2) * seg
        return pltpu.make_async_copy(
            src.at[pl.ds(pl.multiple_of(off, 128), seg)], stage.at[m, r], mat_sem.at[m, r]
        )

    for r in range(8):
        for m in range(2):
            mat_copy(m, r).start()

    state[...] = jnp.zeros_like(state)
    dacc[...] = jnp.zeros_like(dacc)
    hist[...] = jnp.zeros_like(hist)
    scal[0] = jnp.full((8, 128), -1.0, jnp.float32)
    scal[1] = jnp.zeros((8, 128), jnp.float32)

    has = (ix > 0, ix < n_x - 1, iy > 0, iy < n_y - 1)
    peer = ({"sx": ix - 1}, {"sx": ix + 1}, {"sy": iy - 1}, {"sy": iy + 1})
    for d in range(4):
        @pl.when(jnp.logical_not(has[d]))
        def _(d=d):
            frecv[:, d] = jnp.zeros_like(frecv[:, d])

    barrier = pltpu.get_barrier_semaphore()
    for d in range(1, n_x):
        pl.semaphore_signal(barrier, inc=1, device_id={"sx": (ix + d) % n_x}, device_id_type=MESH)
    for d in range(1, n_y):
        pl.semaphore_signal(barrier, inc=1, device_id={"sy": (iy + d) % n_y}, device_id_type=MESH)
    pl.semaphore_signal(barrier, inc=1, device_id={"freq": other}, device_id_type=MESH)
    pl.semaphore_wait(barrier, n_x + n_y - 1)

    def to_partner(src, dst, ssem, rsem):
        return pltpu.make_async_remote_copy(
            src_ref=src, dst_ref=dst, send_sem=ssem, recv_sem=rsem,
            device_id={"freq": other}, device_id_type=MESH,
        )

    prologue = [
        to_partner(ld, ldr, pro_send.at[0], pro_recv.at[0]),
        to_partner(om, omr, pro_send.at[1], pro_recv.at[1]),
        to_partner(st, stb, pro_send.at[2], pro_recv.at[2]),
    ]
    for copy in prologue:
        copy.start()

    row = lax.broadcasted_iota(jnp.int32, (512, 512), 0)
    col = lax.broadcasted_iota(jnp.int32, (512, 512), 1)
    spread = jnp.where(row == 4 * (col % 128) + col // 128, 1.0, 0.0).astype(jnp.bfloat16)

    def place(r, carry):
        rows = pl.ds(pl.multiple_of(r * seg, 128), seg)
        for m in range(2):
            mat_copy(m, r).wait()
            for b in range(blocks):
                moved = jnp.dot(
                    stage[m, r, :, b * 512 : (b + 1) * 512], spread,
                    preferred_element_type=jnp.float32,
                ).astype(jnp.bfloat16)
                for face in range(4):
                    lo = face * seg + b * 128
                    mats[m, rows, lo : lo + 128] = moved[:, face * 128 : (face + 1) * 128]
        return carry

    lax.fori_loop(0, 8, place, 0)

    for copy in prologue:
        copy.wait()
    omw[...] = om[...] + omr[...]
    stw[...] = st[...] + stb[...]
    for face in range(4):
        h, k = face // 2, face % 2
        mine = pl.ds(pl.multiple_of(face * face_len + f * seg, 128), seg)
        theirs = pl.ds(pl.multiple_of(face * face_len + other * seg, 128), seg)
        vown[0, h, 0:16, k * seg : (k + 1) * seg] = ld[:, mine] + ldr[:, mine]
        vpart[0, h, 0:16, k * seg : (k + 1) * seg] = ld[:, theirs] + ldr[:, theirs]
    for h in range(2):
        vown[0, h, 16:32] = jnp.zeros((16, half), jnp.bfloat16)
        vpart[0, h, 16:32] = jnp.zeros((16, half), jnp.bfloat16)

    def v_copy(t, h):
        return to_partner(vown.at[t, h], vpart.at[t, h], vs_sem.at[t, h], vr_sem.at[t, h])

    def face_out(t, d):
        return pltpu.make_async_remote_copy(
            src_ref=fsend.at[t, d], dst_ref=frecv.at[t, d ^ 1],
            send_sem=fs_sem.at[t, d], recv_sem=fr_sem.at[t, d ^ 1],
            device_id=peer[d], device_id_type=MESH,
        )

    def face_in(t, d):
        return pltpu.make_async_remote_copy(
            src_ref=fsend.at[t, d], dst_ref=frecv.at[t, d],
            send_sem=fs_sem.at[t, d], recv_sem=fr_sem.at[t, d],
            device_id=peer[d], device_id_type=MESH,
        )

    def send_faces(t, h):
        for k in range(2):
            d = 2 * h + k
            fsend[t, d] = yloc[h, :, k * seg : (k + 1) * seg]

            @pl.when(has[d])
            def _(d=d):
                face_out(t, d).start()

    def take_faces(t, h):
        for k in range(2):
            d = 2 * h + k

            @pl.when(has[d])
            def _(d=d):
                face_in(t, d).wait()
        got = jnp.concatenate([frecv[t, 2 * h], frecv[t, 2 * h + 1]], axis=1)
        return yloc[h] + got

    def both(x):
        return jnp.concatenate([x, x], axis=0)[:, :1]

    def lanes(x):
        x = x[0:8] + x[8:16]
        total = x[:, 0:128]
        for b in range(1, blocks):
            total = total + x[:, b * 128 : (b + 1) * 128]
        return total

    def finish_adjoint(t, h):
        u = take_faces(t, h)
        alpha, beta = both(scal[0]), both(scal[1])
        w = u + beta * state[W, h]
        n = state[N, h]
        p = n + beta * state[PD, h]
        state[Q, h] = state[FR, h] + beta * state[Q, h]
        state[PD, h] = p
        state[W, h] = w
        state[SOL, h] = state[SOL, h] + alpha * p
        n = n - alpha * w
        state[N, h] = n
        return n

    def finish_image(t, h):
        fresh = take_faces(t, h)
        state[FR, h] = fresh
        n, q = state[N, h], state[Q, h]
        for k in range(2):
            weight = jnp.where(has[2 * h + k], 0.5, 1.0).astype(jnp.float32)
            cut = slice(k * seg, (k + 1) * seg)
            for i, (a, b) in enumerate(((n, n), (fresh, fresh), (fresh, q))):
                part = weight * lanes(a[:, cut] * b[:, cut])
                dacc[8 * i : 8 * i + 8] = dacc[8 * i : 8 * i + 8] + part
        return fresh

    def pass_on(t, h, value):
        high = value.astype(jnp.bfloat16)
        vown[t, h, 0:16] = high
        vown[t, h, 16:32] = (value - high.astype(jnp.float32)).astype(jnp.bfloat16)
        v_copy(t, h).start()

    def ring_copies(it, buf, axis, me, count, ssem, rsem):
        return [
            pltpu.make_async_remote_copy(
                src_ref=buf.at[it, me], dst_ref=buf.at[it, me],
                send_sem=ssem.at[it, d - 1], recv_sem=rsem.at[it, d - 1],
                device_id={axis: (me + d) % count}, device_id_type=MESH,
            )
            for d in range(1, count)
        ]

    def over_y(it):
        return ring_copies(it, red_y, "sy", iy, n_y, ys_sem, yr_sem)

    def over_x(it):
        return ring_copies(it, red_x, "sx", ix, n_x, xs_sem, xr_sem)

    def over_f(it):
        return [to_partner(red_f.at[it, 0], red_f.at[it, 1], ps_sem.at[it], pr_sem.at[it])]

    def reduce_start(it):
        red_y[it, iy] = dacc[...]
        dacc[...] = jnp.zeros_like(dacc)
        for copy in over_y(it):
            copy.start()

    def reduce_mid(it):
        for copy in over_y(it):
            copy.wait()
        total = red_y[it, 0]
        for j in range(1, n_y):
            total = total + red_y[it, j]
        red_x[it, ix] = total
        for copy in over_x(it):
            copy.start()

    def reduce_last(it):
        for copy in over_x(it):
            copy.wait()
        total = red_x[it, 0]
        for j in range(1, n_x):
            total = total + red_x[it, j]
        red_f[it, 0] = total
        for copy in over_f(it):
            copy.start()

    def reduce_end(it):
        for copy in over_f(it):
            copy.wait()
        total = jnp.sum(red_f[it, 0] + red_f[it, 1], axis=1, keepdims=True)
        total = jnp.broadcast_to(total, (24, 128))
        gamma, norm, cross = total[0:8], total[8:16], total[16:24]
        beta = jnp.where(it > 0, gamma / hist[0], 0.0)
        delta = norm + 2.0 * beta * cross + beta * beta * hist[1]
        hist[0] = gamma
        hist[1] = delta
        scal[0] = gamma / delta
        scal[1] = beta

    def products(v, m, rows, h):
        out = jnp.dot(
            v, mats[m, rows * half : (rows + 1) * half, h * half : (h + 1) * half],
            preferred_element_type=jnp.float32,
        )
        return out[0:16] + out[16:32]

    def apply(t, carry):
        it = t // 2
        adjoint_step = t % 2 == 0
        sign = (2 * (t % 2) - 1).astype(jnp.float32) * LOSS_FACTOR
        v = vown[t, 0]
        for h in range(2):
            for m in range(2):
                acc[m, h] = products(v, m, 0, h)

        @pl.when(jnp.logical_and(adjoint_step, t > 0))
        def _():
            pass_on(t, 1, finish_image(t - 1, 1))
            reduce_start(it - 1)

        @pl.when(jnp.logical_not(adjoint_step))
        def _():
            pass_on(t, 1, finish_adjoint(t - 1, 1))

        v = vown[t, 1]
        for h in range(2):
            for m in range(2):
                acc[m, h] = acc[m, h] + products(v, m, 1, h)

        @pl.when(t > 0)
        def _():
            for h in range(2):
                v_copy(t, h).wait()

        @pl.when(jnp.logical_and(adjoint_step, t > 0))
        def _():
            reduce_mid(it - 1)

        omega = both(omw[...])[0:8]
        for h in range(2):
            stiff_part, mass_part = (
                acc[m, h] + products(vpart[t, 0], m, 2, h) + products(vpart[t, 1], m, 3, h)
                for m in range(2)
            )
            yloc[h, 0:8] = stiff_part[0:8] - sign * stiff_part[8:16] - omega * mass_part[0:8]
            yloc[h, 8:16] = stiff_part[8:16] + sign * stiff_part[0:8] - omega * mass_part[8:16]
            send_faces(t, h)
            if h == 0:
                @pl.when(jnp.logical_and(adjoint_step, t > 0))
                def _():
                    reduce_last(it - 1)

        @pl.when(jnp.logical_and(adjoint_step, t > 0))
        def _():
            reduce_end(it - 1)

        @pl.when(adjoint_step)
        def _():
            pass_on(t + 1, 0, finish_adjoint(t, 0))

        @pl.when(jnp.logical_not(adjoint_step))
        def _():
            fresh = finish_image(t, 0)

            @pl.when(t < 2 * ITERS - 1)
            def _():
                pass_on(t + 1, 0, fresh)

        return carry

    lax.fori_loop(0, 2 * ITERS, apply, 0)

    finish_image(2 * ITERS - 1, 1)
    reduce_start(ITERS - 1)
    reduce_mid(ITERS - 1)
    reduce_last(ITERS - 1)
    reduce_end(ITERS - 1)
    out_lvl[...] = jnp.log(hist[0] / cells)
    alpha, beta = both(scal[0]), both(scal[1])
    for h in range(2):
        state[SOL, h] = state[SOL, h] + alpha * (state[N, h] + beta * state[PD, h])
    sol_copy = to_partner(state.at[SOL], solr, epi_send.at[0], epi_recv.at[0])
    sol_copy.start()

    bins = jnp.zeros((16, 128), jnp.float32)
    for face in range(4):
        h, k = face // 2, face % 2
        lam = state[SOL, h, :, k * seg : (k + 1) * seg]
        mine = pl.ds(pl.multiple_of(face * face_len + f * seg, 128), seg)
        u = stw[:, mine].astype(jnp.float32)
        lr, li, ur, ui = lam[0:8], lam[8:16], u[0:8], u[8:16]
        term = lr * ur - li * ui - LOSS_FACTOR * (lr * ui + li * ur)
        dof = jnp.sum(term, axis=0, keepdims=True)
        owner = own[face : face + 1, pl.ds(pl.multiple_of(f * seg, 128), seg)]
        high = lax.broadcasted_iota(jnp.int32, (16, seg), 0) == owner // 128
        low = lax.broadcasted_iota(jnp.int32, (128, seg), 0) == owner % 128
        low = jnp.where(low, 1.0, 0.0).astype(jnp.bfloat16)
        rest = jnp.where(high, dof, 0.0)
        for _ in range(3):
            piece = rest.astype(jnp.bfloat16)
            bins = bins + lax.dot_general(
                piece, low, (((1,), (1,)), ((), ())), preferred_element_type=jnp.float32
            )
            rest = rest - piece.astype(jnp.float32)
    gsend[...] = -grad_factor * bins
    grad_copy = to_partner(gsend, grecv, epi_send.at[1], epi_recv.at[1])
    grad_copy.start()
    for face in range(4):
        h, k = face // 2, face % 2
        mine = pl.ds(pl.multiple_of(face * face_len + f * seg, 128), seg)
        out_sol[:, mine] = state[SOL, h, :, k * seg : (k + 1) * seg]
    sol_copy.wait()
    for face in range(4):
        h, k = face // 2, face % 2
        theirs = pl.ds(pl.multiple_of(face * face_len + other * seg, 128), seg)
        out_sol[:, theirs] = solr[h, :, k * seg : (k + 1) * seg]
    grad_copy.wait()
    out_grad[...] = gsend[...] + grecv[...]


def fused_body(n_x, n_y, stiffness, mass_matrix, omega_table, assignment, adjoint_load, forward_state, owner_index):
    f = lax.axis_index("freq")
    slots = adjoint_load.shape[2]
    face_len = adjoint_load.shape[5]
    order = 4 * face_len
    seg = face_len // 2
    matches = assignment[:, None] == jnp.arange(omega_table.shape[0], dtype=jnp.int32)[None, :]
    slot_omega = jnp.sum(jnp.where(matches, omega_table[None, :], 0.0), axis=1)
    here = lax.broadcasted_iota(jnp.int32, (1, 2, 1, 1), 1) == f

    def all_rows(x):
        x = jnp.swapaxes(x[0, 0].astype(jnp.bfloat16), 0, 1).reshape(2, 1, slots, order)
        return jnp.where(here, x, 0).reshape(4 * slots, order)

    om = jnp.where(here[0, :, :, 0], slot_omega[None, :], 0.0).reshape(2 * slots, 1)
    om = jnp.broadcast_to(om, (2 * slots, 128))
    f32, bf16 = jnp.float32, jnp.bfloat16
    steps = 2 * ITERS
    half = 2 * seg
    dma = pltpu.SemaphoreType.DMA
    vmem = pl.BlockSpec(memory_space=pltpu.VMEM)
    hbm = pl.BlockSpec(memory_space=pl.ANY)
    grad_factor = (DE_SUB / (2 * slots * order)) ** 0.5
    sizes = (n_x, n_y, face_len, float(n_x * n_y * 2 * order), grad_factor)
    sol, grad, level = pl.pallas_call(
        functools.partial(fused_kernel, sizes),
        out_shape=(
            jax.ShapeDtypeStruct((16, order), f32),
            jax.ShapeDtypeStruct((16, 128), f32),
            jax.ShapeDtypeStruct((8, 128), f32),
        ),
        in_specs=[vmem, vmem, vmem, vmem, hbm, hbm],
        out_specs=(vmem, vmem, vmem),
        scratch_shapes=[
            pltpu.VMEM((2, 8, seg, half * 2), bf16),
            pltpu.VMEM((2, order, half * 2), bf16),
            pltpu.VMEM((2, 2, 16, half), f32),
            pltpu.VMEM((steps, 2, 32, half), bf16),
            pltpu.VMEM((steps, 2, 32, half), bf16),
            pltpu.VMEM((steps, 4, 16, seg), f32),
            pltpu.VMEM((steps, 4, 16, seg), f32),
            pltpu.VMEM((6, 2, 16, half), f32),
            pltpu.VMEM((2, 16, half), f32),
            pltpu.VMEM((24, 128), f32),
            pltpu.VMEM((2, 8, 128), f32),
            pltpu.VMEM((2, 8, 128), f32),
            pltpu.VMEM((ITERS, n_y, 24, 128), f32),
            pltpu.VMEM((ITERS, n_x, 24, 128), f32),
            pltpu.VMEM((ITERS, 2, 24, 128), f32),
            pltpu.VMEM((16, order), bf16),
            pltpu.VMEM((16, order), bf16),
            pltpu.VMEM((16, order), bf16),
            pltpu.VMEM((8, 128), f32),
            pltpu.VMEM((8, 128), f32),
            pltpu.VMEM((2, 16, half), f32),
            pltpu.VMEM((16, 128), f32),
            pltpu.VMEM((16, 128), f32),
            dma((2, 8)), dma((3,)), dma((3,)),
            dma((steps, 2)), dma((steps, 2)), dma((steps, 4)), dma((steps, 4)),
            dma((ITERS, n_y - 1)), dma((ITERS, n_y - 1)),
            dma((ITERS, n_x - 1)), dma((ITERS, n_x - 1)),
            dma((ITERS,)), dma((ITERS,)), dma((2,)), dma((2,)),
        ],
        compiler_params=pltpu.CompilerParams(
            collective_id=0, has_side_effects=True, vmem_limit_bytes=50 * 1024 * 1024
        ),
    )(all_rows(adjoint_load), all_rows(forward_state), om, owner_index[0, 0],
      stiffness[0, 0], mass_matrix[0, 0])
    sol = sol.reshape(2, 2, slots, 4, face_len)
    sol = lax.dynamic_index_in_dim(sol, f, axis=1, keepdims=False)
    sol = jnp.swapaxes(sol, 0, 1)[None, None]
    share = DE_SUB // 2
    grad = lax.dynamic_slice_in_dim(grad.reshape(-1), f * share, share, axis=0)
    level = lax.dynamic_slice_in_dim(level[:, 0], f * slots, slots, axis=0)
    return sol, grad[None, None], level


def fits(mesh):
    return mesh.shape["freq"] == 2 and mesh.shape["sx"] > 1 and mesh.shape["sy"] > 1


def solution(mesh):
    if fits(mesh):
        run = functools.partial(fused_body, mesh.shape["sx"], mesh.shape["sy"])
    else:
        run = body
    return jax.shard_map(
        run,
        mesh=mesh,
        in_specs=(
            P("sx", "sy", None, "freq"),
            P("sx", "sy", None, "freq"),
            P(),
            P("freq"),
            P("sx", "sy", "freq", None, None, None),
            P("sx", "sy", "freq", None, None, None),
            P("sx", "sy", None, None),
        ),
        out_specs=(P("sx", "sy", "freq", None, None, None), P("sx", "sy", "freq"), P("freq")),
        check_vma=False,
    )
```

```python
import functools

import jax
import jax.numpy as jnp
from jax import lax
from jax.experimental import pallas as pl
from jax.experimental.pallas import tpu as pltpu
from jax.sharding import PartitionSpec as P

ITERS = 4
DE_SUB = 1728


LOSS_FACTOR = 0.3


def padded(cells, sides, width):
    for axis, dim in sides:
        count = lax.axis_size(axis)
        ends = count - 1
        head = lax.slice_in_dim(cells, 0, width, axis=dim)
        tail = lax.slice_in_dim(cells, cells.shape[dim] - width, cells.shape[dim], axis=dim)
        cells = jnp.concatenate(
            [
                lax.ppermute(tail, axis, [(i, (i + 1) % count) for i in range(ends)]),
                cells,
                lax.ppermute(head, axis, [((i + 1) % count, i) for i in range(ends)]),
            ],
            axis=dim,
        )
    return cells


def face_weights():
    index_x = lax.axis_index("sx")
    size_x = lax.axis_size("sx")
    index_y = lax.axis_index("sy")
    size_y = lax.axis_size("sy")
    west_weight = jnp.where(index_x > 0, 0.5, 1.0)
    east_weight = jnp.where(index_x < size_x - 1, 0.5, 1.0)
    south_weight = jnp.where(index_y > 0, 0.5, 1.0)
    north_weight = jnp.where(index_y < size_y - 1, 0.5, 1.0)
    return jnp.stack([west_weight, east_weight, south_weight, north_weight]).astype(jnp.float32)


def assemble(local_vals):
    padded_x = padded(local_vals[:, :, 0:2].astype(jnp.bfloat16), (("sx", 2),), 1).astype(
        jnp.float32
    )
    padded_y = padded(local_vals[:, :, 2:4].astype(jnp.bfloat16), (("sy", 2),), 1).astype(
        jnp.float32
    )
    west_face = padded_x[:, :, 1] + padded_x[:, :, 0]
    east_face = padded_x[:, :, 2] + padded_x[:, :, 3]
    south_face = padded_y[:, :, 1] + padded_y[:, :, 0]
    north_face = padded_y[:, :, 2] + padded_y[:, :, 3]
    return jnp.stack([west_face, east_face, south_face, north_face], axis=2)


def mix_parts(stiff_part, mass_part, omega_sq, sign_factor):
    factor = omega_sq[:, None, None]
    real_part = (
        stiff_part[:, 0] - sign_factor * LOSS_FACTOR * stiff_part[:, 1] - factor * mass_part[:, 0]
    )
    imag_part = (
        stiff_part[:, 1] + sign_factor * LOSS_FACTOR * stiff_part[:, 0] - factor * mass_part[:, 1]
    )
    return jnp.stack([real_part, imag_part], axis=1)


def apply_rows(vector, stiff_cols, mass_cols, omega_every, sign_factor):
    face_count = vector.shape[2]
    matrix_order = face_count * vector.shape[3]
    rounded = vector.astype(jnp.bfloat16)
    pieces = lax.all_gather(rounded, "freq", axis=0, tiled=True)
    count = pieces.shape[0]
    flattened = pieces.reshape(-1, matrix_order)
    stiff_part = jnp.dot(flattened, stiff_cols, preferred_element_type=jnp.float32)
    mass_part = jnp.dot(flattened, mass_cols, preferred_element_type=jnp.float32)
    local_vals = mix_parts(
        stiff_part.reshape(count, 2, face_count, -1),
        mass_part.reshape(count, 2, face_count, -1),
        omega_every,
        sign_factor,
    )
    returned = lax.all_to_all(
        local_vals.astype(jnp.bfloat16), "freq", split_axis=0, concat_axis=3, tiled=True
    ).astype(local_vals.dtype)
    return assemble(returned)


def reduce_dots(factor_pairs, weights):
    partial_value = tuple(
        (
            jnp.sum(first_vec * second_vec * weights[None, None, :, None], axis=(1, 2, 3))
            for first_vec, second_vec in factor_pairs
        )
    )
    summed = lax.psum(partial_value, ("sx", "sy"))
    return summed


def per_freq(values):
    return values[:, None, None, None]


def face_columns(matrix, matrix_order, face_count):
    grouped = matrix.reshape(matrix_order, -1, face_count)
    return jnp.swapaxes(grouped, 1, 2).reshape(matrix_order, -1)


def body(stiffness, mass_matrix, omega_table, assignment, adjoint_load, forward_state, owner_index):
    n_freq = lax.axis_size("freq")
    slot_count = adjoint_load.shape[2]
    face_count = adjoint_load.shape[4]
    face_len = adjoint_load.shape[5]
    matrix_order = face_count * face_len
    stiff_cols = face_columns(stiffness[0, 0], matrix_order, face_count)
    mass_cols = face_columns(mass_matrix[0, 0], matrix_order, face_count)
    matches = assignment[:, None] == jnp.arange(omega_table.shape[0], dtype=jnp.int32)[None, :]
    slot_omega = jnp.sum(jnp.where(matches, omega_table[None, :], 0.0), axis=1)
    weights = face_weights()
    load_rows = adjoint_load[0, 0]
    omega_every = lax.all_gather(slot_omega, "freq", axis=0, tiled=True)

    def operate(vector, sign_factor):
        return apply_rows(vector, stiff_cols, mass_cols, omega_every, sign_factor)

    residual = load_rows
    solution = jnp.zeros_like(load_rows)
    normal_res = operate(residual, -1.0)
    direction = normal_res
    image_vec = operate(normal_res, 1.0)
    gamma_now, delta_now = reduce_dots(((normal_res, normal_res), (image_vec, image_vec)), weights)
    for iteration in range(ITERS):
        step_size = gamma_now / delta_now
        solution = solution + per_freq(step_size) * direction
        if iteration + 1 < ITERS:
            residual = residual - per_freq(step_size) * image_vec
            normal_res = operate(residual, -1.0)
            fresh = operate(normal_res, 1.0)
            gamma_next, fresh_norm, fresh_cross = reduce_dots(
                ((normal_res, normal_res), (fresh, fresh), (fresh, image_vec)), weights
            )
            beta_ratio = gamma_next / gamma_now
            direction = normal_res + per_freq(beta_ratio) * direction
            image_vec = fresh + per_freq(beta_ratio) * image_vec
            delta_now = (
                fresh_norm + 2.0 * beta_ratio * fresh_cross + beta_ratio * beta_ratio * delta_now
            )
            gamma_now = gamma_next
    cell_count = float(lax.axis_size("sx") * lax.axis_size("sy") * 2 * matrix_order)
    residual_level = jnp.log(gamma_now / cell_count)
    state_vec = forward_state[0, 0].astype(jnp.float32)
    lambda_real = solution[:, 0]
    lambda_imag = solution[:, 1]
    state_real = state_vec[:, 0]
    state_imag = state_vec[:, 1]
    product_term = (
        lambda_real * state_real
        - lambda_imag * state_imag
        - LOSS_FACTOR * (lambda_real * state_imag + lambda_imag * state_real)
    )
    dof_total = jnp.sum(product_term, axis=0)
    partial_grad = jax.ops.segment_sum(
        dof_total.reshape(-1), owner_index[0, 0].reshape(-1), num_segments=DE_SUB
    )
    grad_factor = (DE_SUB / (slot_count * n_freq * matrix_order)) ** 0.5
    gradient = lax.psum_scatter(
        -grad_factor * partial_grad, "freq", scatter_dimension=0, tiled=True
    )
    return (solution[None, None], gradient[None, None], residual_level)


MESH = pl.DeviceIdType.MESH


def fused_kernel(
    sizes, ld, st, om, own, stiff, mass, out_sol, out_grad, out_lvl,
    stage, mats, acc, vbuf, ysend, yrecv, frecv, state, dacc, scal, hist,
    red_y, red_x, ldr, stb, stw, omr, omw,
    mat_sem, pro_send, pro_recv, vs_sem, vr_sem, fs_sem, fr_sem,
    ys_sem, yr_sem, xs_sem, xr_sem,
):
    n_x, n_y, face_len, cells, grad_factor = sizes
    seg = face_len // 2
    half = 2 * seg
    blocks = seg // 128
    f = lax.axis_index("freq")
    ix = lax.axis_index("sx")
    iy = lax.axis_index("sy")
    other = 1 - f
    N, PD, Q, W, FR, SOL = range(6)

    def mat_copy(m, r):
        src = stiff if m == 0 else mass
        off = (2 * (r // 4) + r % 2) * face_len + ((f + r // 2) % 2) * seg
        return pltpu.make_async_copy(
            src.at[pl.ds(pl.multiple_of(off, 128), seg)], stage.at[m, r], mat_sem.at[m, r]
        )

    for r in range(8):
        for m in range(2):
            mat_copy(m, r).start()

    state[...] = jnp.zeros_like(state)
    dacc[...] = jnp.zeros_like(dacc)
    hist[...] = jnp.zeros_like(hist)
    scal[0] = jnp.full((8, 128), -1.0, jnp.float32)
    scal[1] = jnp.zeros((8, 128), jnp.float32)

    has = (ix > 0, ix < n_x - 1, iy > 0, iy < n_y - 1)
    peer = ({"sx": ix - 1}, {"sx": ix + 1}, {"sy": iy - 1}, {"sy": iy + 1})
    for d in range(4):
        @pl.when(jnp.logical_not(has[d]))
        def _(d=d):
            frecv[:, :, d] = jnp.zeros_like(frecv[:, :, d])

    barrier = pltpu.get_barrier_semaphore()
    for side in range(2):
        where = {"freq": (f + side) % 2}
        for d in range(1, n_x):
            pl.semaphore_signal(
                barrier, inc=1, device_id={"sx": (ix + d) % n_x, **where}, device_id_type=MESH
            )
        for d in range(1, n_y):
            pl.semaphore_signal(
                barrier, inc=1, device_id={"sy": (iy + d) % n_y, **where}, device_id_type=MESH
            )
    pl.semaphore_signal(barrier, inc=1, device_id={"freq": other}, device_id_type=MESH)
    pl.semaphore_wait(barrier, 2 * (n_x + n_y - 2) + 1)

    def to_partner(src, dst, ssem, rsem):
        return pltpu.make_async_remote_copy(
            src_ref=src, dst_ref=dst, send_sem=ssem, recv_sem=rsem,
            device_id={"freq": other}, device_id_type=MESH,
        )

    prologue = [
        to_partner(ld, ldr, pro_send.at[0], pro_recv.at[0]),
        to_partner(om, omr, pro_send.at[1], pro_recv.at[1]),
        to_partner(st, stb, pro_send.at[2], pro_recv.at[2]),
    ]
    for copy in prologue:
        copy.start()

    row = lax.broadcasted_iota(jnp.int32, (512, 512), 0)
    col = lax.broadcasted_iota(jnp.int32, (512, 512), 1)
    spread = jnp.where(row == 4 * (col % 128) + col // 128, 1.0, 0.0).astype(jnp.bfloat16)

    def place(r, carry):
        rows = pl.ds(pl.multiple_of(r * seg, 128), seg)
        for m in range(2):
            mat_copy(m, r).wait()
            for b in range(blocks):
                moved = jnp.dot(
                    stage[m, r, :, b * 512 : (b + 1) * 512], spread,
                    preferred_element_type=jnp.float32,
                ).astype(jnp.bfloat16)
                for face in range(4):
                    lo = face * seg + b * 128
                    mats[m, rows, lo : lo + 128] = moved[:, face * 128 : (face + 1) * 128]
        return carry

    lax.fori_loop(0, 8, place, 0)

    for copy in prologue:
        copy.wait()
    omw[...] = om[...] + omr[...]
    stw[...] = st[...] + stb[...]
    def pieces(h):
        for j in range(4):
            side, face = j // 2, 2 * h + j % 2
            here = ((f + side) % 2) * seg
            at = pl.ds(pl.multiple_of(face * face_len + here, 128), seg)
            yield face, here, at, slice(j * seg, (j + 1) * seg)

    for h in range(2):
        for _, _, at, cut in pieces(h):
            vbuf[h, 0:16, cut] = ld[:, at] + ldr[:, at]
        vbuf[h, 16:32] = jnp.zeros((16, 2 * half), jnp.bfloat16)

    def y_copy(t, h):
        return to_partner(ysend.at[t, h], yrecv.at[t, h], vs_sem.at[t, h], vr_sem.at[t, h])

    def face_copy(t, side, d, land):
        where = {"freq": (f + side) % 2} if side else {}
        return pltpu.make_async_remote_copy(
            src_ref=ysend.at[t, d // 2, :, pl.ds((d % 2) * seg, seg)],
            dst_ref=frecv.at[t, side, land],
            send_sem=fs_sem.at[t, side, d], recv_sem=fr_sem.at[t, side, land],
            device_id={**peer[d], **where}, device_id_type=MESH,
        )

    def send_values(t, h):
        for d in (2 * h, 2 * h + 1):
            @pl.when(has[d])
            def _(d=d):
                for side in range(2):
                    face_copy(t, side, d, d ^ 1).start()
        y_copy(t, h).start()

    def take_values(t, h):
        for d in (2 * h, 2 * h + 1):
            @pl.when(has[d])
            def _(d=d):
                for side in range(2):
                    face_copy(t, side, d, d).wait()
        y_copy(t, h).wait()
        got = [frecv[t, j // 2, 2 * h + j % 2] for j in range(4)]
        local = jnp.concatenate([ysend[t, h], yrecv[t, h]], axis=1)
        return local + jnp.concatenate(got, axis=1)

    def both(x):
        return jnp.concatenate([x, x], axis=0)[:, :1]

    def lanes(x):
        x = x[0:8] + x[8:16]
        total = x[:, 0:128]
        for b in range(1, blocks):
            total = total + x[:, b * 128 : (b + 1) * 128]
        return total

    def finish_adjoint(t, h):
        u = take_values(t, h)
        alpha, beta = both(scal[0]), both(scal[1])
        w = u + beta * state[W, h]
        n = state[N, h]
        p = n + beta * state[PD, h]
        state[Q, h] = state[FR, h] + beta * state[Q, h]
        state[PD, h] = p
        state[W, h] = w
        state[SOL, h] = state[SOL, h] + alpha * p
        n = n - alpha * w
        state[N, h] = n
        return n

    def finish_image(t, h):
        fresh = take_values(t, h)
        state[FR, h] = fresh
        n, q = state[N, h], state[Q, h]
        for face, _, _, cut in pieces(h):
            weight = jnp.where(has[face], 0.5, 1.0).astype(jnp.float32)
            for i, (a, b) in enumerate(((n, n), (fresh, fresh), (fresh, q))):
                part = weight * lanes(a[:, cut] * b[:, cut])
                dacc[8 * i : 8 * i + 8] = dacc[8 * i : 8 * i + 8] + part
        return fresh

    def pass_on(h, value):
        high = value.astype(jnp.bfloat16)
        vbuf[h, 0:16] = high
        vbuf[h, 16:32] = (value - high.astype(jnp.float32)).astype(jnp.bfloat16)

    def ring_copies(it, buf, axis, me, count, ssem, rsem):
        return [
            pltpu.make_async_remote_copy(
                src_ref=buf.at[it, me], dst_ref=buf.at[it, me],
                send_sem=ssem.at[it, d - 1], recv_sem=rsem.at[it, d - 1],
                device_id={axis: (me + d) % count}, device_id_type=MESH,
            )
            for d in range(1, count)
        ]

    def over_y(it):
        return ring_copies(it, red_y, "sy", iy, n_y, ys_sem, yr_sem)

    def over_x(it):
        return ring_copies(it, red_x, "sx", ix, n_x, xs_sem, xr_sem)

    def reduce_start(it):
        red_y[it, iy] = dacc[...]
        dacc[...] = jnp.zeros_like(dacc)
        for copy in over_y(it):
            copy.start()

    def reduce_mid(it):
        for copy in over_y(it):
            copy.wait()
        total = red_y[it, 0]
        for j in range(1, n_y):
            total = total + red_y[it, j]
        red_x[it, ix] = total
        for copy in over_x(it):
            copy.start()

    def reduce_end(it):
        for copy in over_x(it):
            copy.wait()
        total = red_x[it, 0]
        for j in range(1, n_x):
            total = total + red_x[it, j]
        total = jnp.broadcast_to(jnp.sum(total, axis=1, keepdims=True), (24, 128))
        gamma, norm, cross = total[0:8], total[8:16], total[16:24]
        beta = jnp.where(it > 0, gamma / hist[0], 0.0)
        delta = norm + 2.0 * beta * cross + beta * beta * hist[1]
        hist[0] = gamma
        hist[1] = delta
        scal[0] = gamma / delta
        scal[1] = beta

    def products(m, rows, h):
        out = jnp.dot(
            vbuf[rows],
            mats[m, rows * 2 * half : (rows + 1) * 2 * half, h * half : (h + 1) * half],
            preferred_element_type=jnp.float32,
        )
        return out[0:16] + out[16:32]

    def apply(t, carry):
        it = t // 2
        adjoint_step = t % 2 == 0
        reducing = jnp.logical_and(adjoint_step, t > 0)
        sign = (2 * (t % 2) - 1).astype(jnp.float32) * LOSS_FACTOR
        for h in range(2):
            for m in range(2):
                acc[m, h] = products(m, 0, h)

        @pl.when(reducing)
        def _():
            pass_on(1, finish_image(t - 1, 1))
            reduce_start(it - 1)

        @pl.when(jnp.logical_not(adjoint_step))
        def _():
            pass_on(1, finish_adjoint(t - 1, 1))

        omega = both(omw[...])[0:8]
        for h in range(2):
            stiff_part, mass_part = (acc[m, h] + products(m, 1, h) for m in range(2))
            ysend[t, h, 0:8] = stiff_part[0:8] - sign * stiff_part[8:16] - omega * mass_part[0:8]
            ysend[t, h, 8:16] = stiff_part[8:16] + sign * stiff_part[0:8] - omega * mass_part[8:16]
            send_values(t, h)
            if h == 0:
                @pl.when(reducing)
                def _():
                    reduce_mid(it - 1)

        @pl.when(reducing)
        def _():
            reduce_end(it - 1)

        @pl.when(adjoint_step)
        def _():
            pass_on(0, finish_adjoint(t, 0))

        @pl.when(jnp.logical_not(adjoint_step))
        def _():
            pass_on(0, finish_image(t, 0))

        return carry

    lax.fori_loop(0, 2 * ITERS, apply, 0)

    finish_image(2 * ITERS - 1, 1)
    reduce_start(ITERS - 1)
    reduce_mid(ITERS - 1)
    reduce_end(ITERS - 1)
    out_lvl[...] = jnp.log(hist[0] / cells)
    alpha, beta = both(scal[0]), both(scal[1])
    for h in range(2):
        state[SOL, h] = state[SOL, h] + alpha * (state[N, h] + beta * state[PD, h])

    bins = jnp.zeros((16, 128), jnp.float32)
    for h in range(2):
        for face, here, at, cut in pieces(h):
            lam = state[SOL, h, :, cut]
            out_sol[:, at] = lam
            u = stw[:, at].astype(jnp.float32)
            lr, li, ur, ui = lam[0:8], lam[8:16], u[0:8], u[8:16]
            term = lr * ur - li * ui - LOSS_FACTOR * (lr * ui + li * ur)
            dof = jnp.sum(term, axis=0, keepdims=True)
            owner = own[face : face + 1, pl.ds(pl.multiple_of(here, 128), seg)]
            high = lax.broadcasted_iota(jnp.int32, (16, seg), 0) == owner // 128
            low = lax.broadcasted_iota(jnp.int32, (128, seg), 0) == owner % 128
            low = jnp.where(low, 1.0, 0.0).astype(jnp.bfloat16)
            rest = jnp.where(high, dof, 0.0)
            for _ in range(3):
                piece = rest.astype(jnp.bfloat16)
                bins = bins + lax.dot_general(
                    piece, low, (((1,), (1,)), ((), ())), preferred_element_type=jnp.float32
                )
                rest = rest - piece.astype(jnp.float32)
    out_grad[...] = -grad_factor * bins


def fused_body(n_x, n_y, stiffness, mass_matrix, omega_table, assignment, adjoint_load, forward_state, owner_index):
    f = lax.axis_index("freq")
    slots = adjoint_load.shape[2]
    face_len = adjoint_load.shape[5]
    order = 4 * face_len
    seg = face_len // 2
    matches = assignment[:, None] == jnp.arange(omega_table.shape[0], dtype=jnp.int32)[None, :]
    slot_omega = jnp.sum(jnp.where(matches, omega_table[None, :], 0.0), axis=1)
    here = lax.broadcasted_iota(jnp.int32, (1, 2, 1, 1), 1) == f

    def all_rows(x):
        x = jnp.swapaxes(x[0, 0].astype(jnp.bfloat16), 0, 1).reshape(2, 1, slots, order)
        return jnp.where(here, x, 0).reshape(4 * slots, order)

    om = jnp.where(here[0, :, :, 0], slot_omega[None, :], 0.0).reshape(2 * slots, 1)
    om = jnp.broadcast_to(om, (2 * slots, 128))
    f32, bf16 = jnp.float32, jnp.bfloat16
    steps = 2 * ITERS
    half = 2 * seg
    dma = pltpu.SemaphoreType.DMA
    vmem = pl.BlockSpec(memory_space=pltpu.VMEM)
    hbm = pl.BlockSpec(memory_space=pl.ANY)
    grad_factor = (DE_SUB / (2 * slots * order)) ** 0.5
    sizes = (n_x, n_y, face_len, float(n_x * n_y * 2 * order), grad_factor)
    sol, grad, level = pl.pallas_call(
        functools.partial(fused_kernel, sizes),
        out_shape=(
            jax.ShapeDtypeStruct((16, order), f32),
            jax.ShapeDtypeStruct((16, 128), f32),
            jax.ShapeDtypeStruct((8, 128), f32),
        ),
        in_specs=[vmem, vmem, vmem, vmem, hbm, hbm],
        out_specs=(vmem, vmem, vmem),
        scratch_shapes=[
            pltpu.VMEM((2, 8, seg, half * 2), bf16),
            pltpu.VMEM((2, order, half * 2), bf16),
            pltpu.VMEM((2, 2, 16, half), f32),
            pltpu.VMEM((2, 32, 2 * half), bf16),
            pltpu.VMEM((steps, 2, 16, half), f32),
            pltpu.VMEM((steps, 2, 16, half), f32),
            pltpu.VMEM((steps, 2, 4, 16, seg), f32),
            pltpu.VMEM((6, 2, 16, 2 * half), f32),
            pltpu.VMEM((24, 128), f32),
            pltpu.VMEM((2, 8, 128), f32),
            pltpu.VMEM((2, 8, 128), f32),
            pltpu.VMEM((ITERS, n_y, 24, 128), f32),
            pltpu.VMEM((ITERS, n_x, 24, 128), f32),
            pltpu.VMEM((16, order), bf16),
            pltpu.VMEM((16, order), bf16),
            pltpu.VMEM((16, order), bf16),
            pltpu.VMEM((8, 128), f32),
            pltpu.VMEM((8, 128), f32),
            dma((2, 8)), dma((3,)), dma((3,)),
            dma((steps, 2)), dma((steps, 2)), dma((steps, 2, 4)), dma((steps, 2, 4)),
            dma((ITERS, n_y - 1)), dma((ITERS, n_y - 1)),
            dma((ITERS, n_x - 1)), dma((ITERS, n_x - 1)),
        ],
        compiler_params=pltpu.CompilerParams(
            collective_id=0, has_side_effects=True, vmem_limit_bytes=50 * 1024 * 1024
        ),
    )(all_rows(adjoint_load), all_rows(forward_state), om, owner_index[0, 0],
      stiffness[0, 0], mass_matrix[0, 0])
    sol = sol.reshape(2, 2, slots, 4, face_len)
    sol = lax.dynamic_index_in_dim(sol, f, axis=1, keepdims=False)
    sol = jnp.swapaxes(sol, 0, 1)[None, None]
    share = DE_SUB // 2
    grad = lax.dynamic_slice_in_dim(grad.reshape(-1), f * share, share, axis=0)
    level = lax.dynamic_slice_in_dim(level[:, 0], f * slots, slots, axis=0)
    return sol, grad[None, None], level


def fits(mesh):
    return mesh.shape["freq"] == 2 and mesh.shape["sx"] > 1 and mesh.shape["sy"] > 1


def solution(mesh):
    if fits(mesh):
        run = functools.partial(fused_body, mesh.shape["sx"], mesh.shape["sy"])
    else:
        run = body
    return jax.shard_map(
        run,
        mesh=mesh,
        in_specs=(
            P("sx", "sy", None, "freq"),
            P("sx", "sy", None, "freq"),
            P(),
            P("freq"),
            P("sx", "sy", "freq", None, None, None),
            P("sx", "sy", "freq", None, None, None),
            P("sx", "sy", None, None),
        ),
        out_specs=(P("sx", "sy", "freq", None, None, None), P("sx", "sy", "freq"), P("freq")),
        check_vma=False,
    )
```

```python
import functools

import jax
import jax.numpy as jnp
from jax import lax
from jax.experimental import pallas as pl
from jax.experimental.pallas import tpu as pltpu
from jax.sharding import PartitionSpec as P

ITERS = 4
DE_SUB = 1728


LOSS_FACTOR = 0.3


def padded(cells, sides, width):
    for axis, dim in sides:
        count = lax.axis_size(axis)
        ends = count - 1
        head = lax.slice_in_dim(cells, 0, width, axis=dim)
        tail = lax.slice_in_dim(cells, cells.shape[dim] - width, cells.shape[dim], axis=dim)
        cells = jnp.concatenate(
            [
                lax.ppermute(tail, axis, [(i, (i + 1) % count) for i in range(ends)]),
                cells,
                lax.ppermute(head, axis, [((i + 1) % count, i) for i in range(ends)]),
            ],
            axis=dim,
        )
    return cells


def face_weights():
    index_x = lax.axis_index("sx")
    size_x = lax.axis_size("sx")
    index_y = lax.axis_index("sy")
    size_y = lax.axis_size("sy")
    west_weight = jnp.where(index_x > 0, 0.5, 1.0)
    east_weight = jnp.where(index_x < size_x - 1, 0.5, 1.0)
    south_weight = jnp.where(index_y > 0, 0.5, 1.0)
    north_weight = jnp.where(index_y < size_y - 1, 0.5, 1.0)
    return jnp.stack([west_weight, east_weight, south_weight, north_weight]).astype(jnp.float32)


def assemble(local_vals):
    padded_x = padded(local_vals[:, :, 0:2].astype(jnp.bfloat16), (("sx", 2),), 1).astype(
        jnp.float32
    )
    padded_y = padded(local_vals[:, :, 2:4].astype(jnp.bfloat16), (("sy", 2),), 1).astype(
        jnp.float32
    )
    west_face = padded_x[:, :, 1] + padded_x[:, :, 0]
    east_face = padded_x[:, :, 2] + padded_x[:, :, 3]
    south_face = padded_y[:, :, 1] + padded_y[:, :, 0]
    north_face = padded_y[:, :, 2] + padded_y[:, :, 3]
    return jnp.stack([west_face, east_face, south_face, north_face], axis=2)


def mix_parts(stiff_part, mass_part, omega_sq, sign_factor):
    factor = omega_sq[:, None, None]
    real_part = (
        stiff_part[:, 0] - sign_factor * LOSS_FACTOR * stiff_part[:, 1] - factor * mass_part[:, 0]
    )
    imag_part = (
        stiff_part[:, 1] + sign_factor * LOSS_FACTOR * stiff_part[:, 0] - factor * mass_part[:, 1]
    )
    return jnp.stack([real_part, imag_part], axis=1)


def apply_rows(vector, stiff_cols, mass_cols, omega_every, sign_factor):
    face_count = vector.shape[2]
    matrix_order = face_count * vector.shape[3]
    rounded = vector.astype(jnp.bfloat16)
    pieces = lax.all_gather(rounded, "freq", axis=0, tiled=True)
    count = pieces.shape[0]
    flattened = pieces.reshape(-1, matrix_order)
    stiff_part = jnp.dot(flattened, stiff_cols, preferred_element_type=jnp.float32)
    mass_part = jnp.dot(flattened, mass_cols, preferred_element_type=jnp.float32)
    local_vals = mix_parts(
        stiff_part.reshape(count, 2, face_count, -1),
        mass_part.reshape(count, 2, face_count, -1),
        omega_every,
        sign_factor,
    )
    returned = lax.all_to_all(
        local_vals.astype(jnp.bfloat16), "freq", split_axis=0, concat_axis=3, tiled=True
    ).astype(local_vals.dtype)
    return assemble(returned)


def reduce_dots(factor_pairs, weights):
    partial_value = tuple(
        (
            jnp.sum(first_vec * second_vec * weights[None, None, :, None], axis=(1, 2, 3))
            for first_vec, second_vec in factor_pairs
        )
    )
    summed = lax.psum(partial_value, ("sx", "sy"))
    return summed


def per_freq(values):
    return values[:, None, None, None]


def face_columns(matrix, matrix_order, face_count):
    grouped = matrix.reshape(matrix_order, -1, face_count)
    return jnp.swapaxes(grouped, 1, 2).reshape(matrix_order, -1)


def body(stiffness, mass_matrix, omega_table, assignment, adjoint_load, forward_state, owner_index):
    n_freq = lax.axis_size("freq")
    slot_count = adjoint_load.shape[2]
    face_count = adjoint_load.shape[4]
    face_len = adjoint_load.shape[5]
    matrix_order = face_count * face_len
    stiff_cols = face_columns(stiffness[0, 0], matrix_order, face_count)
    mass_cols = face_columns(mass_matrix[0, 0], matrix_order, face_count)
    matches = assignment[:, None] == jnp.arange(omega_table.shape[0], dtype=jnp.int32)[None, :]
    slot_omega = jnp.sum(jnp.where(matches, omega_table[None, :], 0.0), axis=1)
    weights = face_weights()
    load_rows = adjoint_load[0, 0]
    omega_every = lax.all_gather(slot_omega, "freq", axis=0, tiled=True)

    def operate(vector, sign_factor):
        return apply_rows(vector, stiff_cols, mass_cols, omega_every, sign_factor)

    residual = load_rows
    solution = jnp.zeros_like(load_rows)
    normal_res = operate(residual, -1.0)
    direction = normal_res
    image_vec = operate(normal_res, 1.0)
    gamma_now, delta_now = reduce_dots(((normal_res, normal_res), (image_vec, image_vec)), weights)
    for iteration in range(ITERS):
        step_size = gamma_now / delta_now
        solution = solution + per_freq(step_size) * direction
        if iteration + 1 < ITERS:
            residual = residual - per_freq(step_size) * image_vec
            normal_res = operate(residual, -1.0)
            fresh = operate(normal_res, 1.0)
            gamma_next, fresh_norm, fresh_cross = reduce_dots(
                ((normal_res, normal_res), (fresh, fresh), (fresh, image_vec)), weights
            )
            beta_ratio = gamma_next / gamma_now
            direction = normal_res + per_freq(beta_ratio) * direction
            image_vec = fresh + per_freq(beta_ratio) * image_vec
            delta_now = (
                fresh_norm + 2.0 * beta_ratio * fresh_cross + beta_ratio * beta_ratio * delta_now
            )
            gamma_now = gamma_next
    cell_count = float(lax.axis_size("sx") * lax.axis_size("sy") * 2 * matrix_order)
    residual_level = jnp.log(gamma_now / cell_count)
    state_vec = forward_state[0, 0].astype(jnp.float32)
    lambda_real = solution[:, 0]
    lambda_imag = solution[:, 1]
    state_real = state_vec[:, 0]
    state_imag = state_vec[:, 1]
    product_term = (
        lambda_real * state_real
        - lambda_imag * state_imag
        - LOSS_FACTOR * (lambda_real * state_imag + lambda_imag * state_real)
    )
    dof_total = jnp.sum(product_term, axis=0)
    partial_grad = jax.ops.segment_sum(
        dof_total.reshape(-1), owner_index[0, 0].reshape(-1), num_segments=DE_SUB
    )
    grad_factor = (DE_SUB / (slot_count * n_freq * matrix_order)) ** 0.5
    gradient = lax.psum_scatter(
        -grad_factor * partial_grad, "freq", scatter_dimension=0, tiled=True
    )
    return (solution[None, None], gradient[None, None], residual_level)


MESH = pl.DeviceIdType.MESH
NROWS = 128


def fused_kernel(
    sizes, ld, st, om, own, stiff, mass, out_sol, out_grad, out_lvl,
    stage, mats, acc, vbuf, ysend, yrecv, frecv, state, dacc, scal, hist,
    red_y, red_x, ldr, stb, stw, omr, omw,
    mat_sem, pro_send, pro_recv, vs_sem, vr_sem, fs_sem, fr_sem,
    ys_sem, yr_sem, xs_sem, xr_sem,
):
    n_x, n_y, face_len, cells, grad_factor = sizes
    seg = face_len // 2
    half = 2 * seg
    blocks = seg // 128
    f = lax.axis_index("freq")
    ix = lax.axis_index("sx")
    iy = lax.axis_index("sy")
    other = 1 - f
    N, PD, Q, W, FR, SOL = range(6)

    def mat_copy(m, r):
        src = stiff if m == 0 else mass
        off = (2 * (r // 4) + r % 2) * face_len + ((f + r // 2) % 2) * seg
        return pltpu.make_async_copy(
            src.at[pl.ds(pl.multiple_of(off, 128), seg)], stage.at[m, r], mat_sem.at[m, r]
        )

    for r in range(8):
        for m in range(2):
            mat_copy(m, r).start()

    state[...] = jnp.zeros_like(state)
    vbuf[...] = jnp.zeros_like(vbuf)
    dacc[...] = jnp.zeros_like(dacc)
    hist[...] = jnp.zeros_like(hist)
    scal[0] = jnp.full((8, 128), -1.0, jnp.float32)
    scal[1] = jnp.zeros((8, 128), jnp.float32)

    has = (ix > 0, ix < n_x - 1, iy > 0, iy < n_y - 1)
    peer = ({"sx": ix - 1}, {"sx": ix + 1}, {"sy": iy - 1}, {"sy": iy + 1})
    for d in range(4):
        @pl.when(jnp.logical_not(has[d]))
        def _(d=d):
            frecv[:, :, d] = jnp.zeros_like(frecv[:, :, d])

    barrier = pltpu.get_barrier_semaphore()
    for side in range(2):
        where = {"freq": (f + side) % 2}
        for d in range(1, n_x):
            pl.semaphore_signal(
                barrier, inc=1, device_id={"sx": (ix + d) % n_x, **where}, device_id_type=MESH
            )
        for d in range(1, n_y):
            pl.semaphore_signal(
                barrier, inc=1, device_id={"sy": (iy + d) % n_y, **where}, device_id_type=MESH
            )
    pl.semaphore_signal(barrier, inc=1, device_id={"freq": other}, device_id_type=MESH)
    pl.semaphore_wait(barrier, 2 * (n_x + n_y - 2) + 1)

    def to_partner(src, dst, ssem, rsem):
        return pltpu.make_async_remote_copy(
            src_ref=src, dst_ref=dst, send_sem=ssem, recv_sem=rsem,
            device_id={"freq": other}, device_id_type=MESH,
        )

    prologue = [
        to_partner(ld, ldr, pro_send.at[0], pro_recv.at[0]),
        to_partner(om, omr, pro_send.at[1], pro_recv.at[1]),
        to_partner(st, stb, pro_send.at[2], pro_recv.at[2]),
    ]
    for copy in prologue:
        copy.start()

    row = lax.broadcasted_iota(jnp.int32, (512, 512), 0)
    col = lax.broadcasted_iota(jnp.int32, (512, 512), 1)
    spread = jnp.where(col == 4 * (row % 128) + row // 128, 1.0, 0.0).astype(jnp.bfloat16)

    def place(r, carry):
        rows = pl.ds(pl.multiple_of(r * seg, 128), seg)
        for m in range(2):
            mat_copy(m, r).wait()
            for b in range(blocks):
                moved = lax.dot_general(
                    spread, stage[m, r, :, b * 512 : (b + 1) * 512], (((1,), (1,)), ((), ())),
                    preferred_element_type=jnp.float32,
                ).astype(jnp.bfloat16)
                for face in range(4):
                    lo = face * seg + b * 128
                    mats[m, lo : lo + 128, rows] = moved[face * 128 : (face + 1) * 128]
        return carry

    lax.fori_loop(0, 8, place, 0)

    for copy in prologue:
        copy.wait()
    omw[...] = om[...] + omr[...]
    stw[...] = st[...] + stb[...]
    def pieces(h):
        for j in range(4):
            side, face = j // 2, 2 * h + j % 2
            here = ((f + side) % 2) * seg
            at = pl.ds(pl.multiple_of(face * face_len + here, 128), seg)
            yield face, here, at, slice(j * seg, (j + 1) * seg)

    for h in range(2):
        for _, _, at, cut in pieces(h):
            start = ld[:, at] + ldr[:, at]
            vbuf[h, 0, 0:16, cut] = start
            vbuf[h, 1, 32:48, cut] = start

    def y_copy(t, h):
        return to_partner(ysend.at[t, h], yrecv.at[t, h], vs_sem.at[t, h], vr_sem.at[t, h])

    def face_copy(t, side, d, land):
        where = {"freq": (f + side) % 2} if side else {}
        return pltpu.make_async_remote_copy(
            src_ref=ysend.at[t, d // 2, :, pl.ds((d % 2) * seg, seg)],
            dst_ref=frecv.at[t, side, land],
            send_sem=fs_sem.at[t, side, d], recv_sem=fr_sem.at[t, side, land],
            device_id={**peer[d], **where}, device_id_type=MESH,
        )

    def send_values(t, h):
        for d in (2 * h, 2 * h + 1):
            @pl.when(has[d])
            def _(d=d):
                for side in range(2):
                    face_copy(t, side, d, d ^ 1).start()
        y_copy(t, h).start()

    def take_values(t, h):
        for d in (2 * h, 2 * h + 1):
            @pl.when(has[d])
            def _(d=d):
                for side in range(2):
                    face_copy(t, side, d, d).wait()
        y_copy(t, h).wait()
        got = [frecv[t, j // 2, 2 * h + j % 2] for j in range(4)]
        local = jnp.concatenate([ysend[t, h], yrecv[t, h]], axis=1)
        return local + jnp.concatenate(got, axis=1)

    def both(x):
        return jnp.concatenate([x, x], axis=0)[:, :1]

    def lanes(x):
        x = x[0:8] + x[8:16]
        total = x[:, 0:128]
        for b in range(1, blocks):
            total = total + x[:, b * 128 : (b + 1) * 128]
        return total

    def finish_adjoint(t, h):
        u = take_values(t, h)
        alpha, beta = both(scal[0]), both(scal[1])
        w = u + beta * state[W, h]
        n = state[N, h]
        p = n + beta * state[PD, h]
        state[Q, h] = state[FR, h] + beta * state[Q, h]
        state[PD, h] = p
        state[W, h] = w
        state[SOL, h] = state[SOL, h] + alpha * p
        n = n - alpha * w
        state[N, h] = n
        return n

    def finish_image(t, h):
        fresh = take_values(t, h)
        state[FR, h] = fresh
        n, q = state[N, h], state[Q, h]
        for face, _, _, cut in pieces(h):
            weight = jnp.where(has[face], 0.5, 1.0).astype(jnp.float32)
            for i, (a, b) in enumerate(((n, n), (fresh, fresh), (fresh, q))):
                part = weight * lanes(a[:, cut] * b[:, cut])
                dacc[8 * i : 8 * i + 8] = dacc[8 * i : 8 * i + 8] + part
        return fresh

    def pass_on(h, value):
        high = value.astype(jnp.bfloat16)
        low = (value - high.astype(jnp.float32)).astype(jnp.bfloat16)
        for m in range(2):
            vbuf[h, m, 32 * m : 32 * m + 16] = high
            vbuf[h, m, 32 * m + 16 : 32 * m + 32] = low

    def ring_copies(it, buf, axis, me, count, ssem, rsem):
        return [
            pltpu.make_async_remote_copy(
                src_ref=buf.at[it, me], dst_ref=buf.at[it, me],
                send_sem=ssem.at[it, d - 1], recv_sem=rsem.at[it, d - 1],
                device_id={axis: (me + d) % count}, device_id_type=MESH,
            )
            for d in range(1, count)
        ]

    def over_y(it):
        return ring_copies(it, red_y, "sy", iy, n_y, ys_sem, yr_sem)

    def over_x(it):
        return ring_copies(it, red_x, "sx", ix, n_x, xs_sem, xr_sem)

    def reduce_start(it):
        red_y[it, iy] = dacc[...]
        dacc[...] = jnp.zeros_like(dacc)
        for copy in over_y(it):
            copy.start()

    def reduce_mid(it):
        for copy in over_y(it):
            copy.wait()
        total = red_y[it, 0]
        for j in range(1, n_y):
            total = total + red_y[it, j]
        red_x[it, ix] = total
        for copy in over_x(it):
            copy.start()

    def reduce_end(it):
        for copy in over_x(it):
            copy.wait()
        total = red_x[it, 0]
        for j in range(1, n_x):
            total = total + red_x[it, j]
        total = jnp.broadcast_to(jnp.sum(total, axis=1, keepdims=True), (24, 128))
        gamma, norm, cross = total[0:8], total[8:16], total[16:24]
        beta = jnp.where(it > 0, gamma / hist[0], 0.0)
        delta = norm + 2.0 * beta * cross + beta * beta * hist[1]
        hist[0] = gamma
        hist[1] = delta
        scal[0] = gamma / delta
        scal[1] = beta

    def products(rows, h):
        out = [
            lax.dot_general(
                mats[m, h * half : (h + 1) * half, rows * 2 * half : (rows + 1) * 2 * half],
                vbuf[rows, m], (((1,), (1,)), ((), ())),
                preferred_element_type=jnp.float32,
            )
            for m in range(2)
        ]
        return out[0] + out[1]

    def apply(t, carry):
        it = t // 2
        adjoint_step = t % 2 == 0
        reducing = jnp.logical_and(adjoint_step, t > 0)
        sign = (2 * (t % 2) - 1).astype(jnp.float32) * LOSS_FACTOR
        for h in range(2):
            acc[h] = products(0, h)

        @pl.when(reducing)
        def _():
            pass_on(1, finish_image(t - 1, 1))
            reduce_start(it - 1)

        @pl.when(jnp.logical_not(adjoint_step))
        def _():
            pass_on(1, finish_adjoint(t - 1, 1))

        omega = both(omw[...])[0:8]
        for h in range(2):
            done = jnp.transpose(acc[h] + products(1, h))
            stiff_part = done[0:16] + done[16:32]
            mass_part = done[32:48] + done[48:64]
            ysend[t, h, 0:8] = stiff_part[0:8] - sign * stiff_part[8:16] - omega * mass_part[0:8]
            ysend[t, h, 8:16] = stiff_part[8:16] + sign * stiff_part[0:8] - omega * mass_part[8:16]
            send_values(t, h)
            if h == 0:
                @pl.when(reducing)
                def _():
                    reduce_mid(it - 1)

        @pl.when(reducing)
        def _():
            reduce_end(it - 1)

        @pl.when(adjoint_step)
        def _():
            pass_on(0, finish_adjoint(t, 0))

        @pl.when(jnp.logical_not(adjoint_step))
        def _():
            pass_on(0, finish_image(t, 0))

        return carry

    lax.fori_loop(0, 2 * ITERS, apply, 0)

    finish_image(2 * ITERS - 1, 1)
    reduce_start(ITERS - 1)
    reduce_mid(ITERS - 1)
    reduce_end(ITERS - 1)
    out_lvl[...] = jnp.log(hist[0] / cells)
    alpha, beta = both(scal[0]), both(scal[1])
    for h in range(2):
        state[SOL, h] = state[SOL, h] + alpha * (state[N, h] + beta * state[PD, h])

    bins = jnp.zeros((16, 128), jnp.float32)
    for h in range(2):
        for face, here, at, cut in pieces(h):
            lam = state[SOL, h, :, cut]
            out_sol[:, at] = lam
            u = stw[:, at].astype(jnp.float32)
            lr, li, ur, ui = lam[0:8], lam[8:16], u[0:8], u[8:16]
            term = lr * ur - li * ui - LOSS_FACTOR * (lr * ui + li * ur)
            dof = jnp.sum(term, axis=0, keepdims=True)
            owner = own[face : face + 1, pl.ds(pl.multiple_of(here, 128), seg)]
            high = lax.broadcasted_iota(jnp.int32, (16, seg), 0) == owner // 128
            low = lax.broadcasted_iota(jnp.int32, (128, seg), 0) == owner % 128
            low = jnp.where(low, 1.0, 0.0).astype(jnp.bfloat16)
            rest = jnp.where(high, dof, 0.0)
            for _ in range(3):
                piece = rest.astype(jnp.bfloat16)
                bins = bins + lax.dot_general(
                    piece, low, (((1,), (1,)), ((), ())), preferred_element_type=jnp.float32
                )
                rest = rest - piece.astype(jnp.float32)
    out_grad[...] = -grad_factor * bins


def fused_body(n_x, n_y, stiffness, mass_matrix, omega_table, assignment, adjoint_load, forward_state, owner_index):
    f = lax.axis_index("freq")
    slots = adjoint_load.shape[2]
    face_len = adjoint_load.shape[5]
    order = 4 * face_len
    seg = face_len // 2
    matches = assignment[:, None] == jnp.arange(omega_table.shape[0], dtype=jnp.int32)[None, :]
    slot_omega = jnp.sum(jnp.where(matches, omega_table[None, :], 0.0), axis=1)
    here = lax.broadcasted_iota(jnp.int32, (1, 2, 1, 1), 1) == f

    def all_rows(x):
        x = jnp.swapaxes(x[0, 0].astype(jnp.bfloat16), 0, 1).reshape(2, 1, slots, order)
        return jnp.where(here, x, 0).reshape(4 * slots, order)

    om = jnp.where(here[0, :, :, 0], slot_omega[None, :], 0.0).reshape(2 * slots, 1)
    om = jnp.broadcast_to(om, (2 * slots, 128))
    f32, bf16 = jnp.float32, jnp.bfloat16
    steps = 2 * ITERS
    half = 2 * seg
    dma = pltpu.SemaphoreType.DMA
    vmem = pl.BlockSpec(memory_space=pltpu.VMEM)
    hbm = pl.BlockSpec(memory_space=pl.ANY)
    grad_factor = (DE_SUB / (2 * slots * order)) ** 0.5
    sizes = (n_x, n_y, face_len, float(n_x * n_y * 2 * order), grad_factor)
    sol, grad, level = pl.pallas_call(
        functools.partial(fused_kernel, sizes),
        out_shape=(
            jax.ShapeDtypeStruct((16, order), f32),
            jax.ShapeDtypeStruct((16, 128), f32),
            jax.ShapeDtypeStruct((8, 128), f32),
        ),
        in_specs=[vmem, vmem, vmem, vmem, hbm, hbm],
        out_specs=(vmem, vmem, vmem),
        scratch_shapes=[
            pltpu.VMEM((2, 8, seg, half * 2), bf16),
            pltpu.VMEM((2, half * 2, order), bf16),
            pltpu.VMEM((2, half, NROWS), f32),
            pltpu.VMEM((2, 2, NROWS, 2 * half), bf16),
            pltpu.VMEM((steps, 2, 16, half), f32),
            pltpu.VMEM((steps, 2, 16, half), f32),
            pltpu.VMEM((steps, 2, 4, 16, seg), f32),
            pltpu.VMEM((6, 2, 16, 2 * half), f32),
            pltpu.VMEM((24, 128), f32),
            pltpu.VMEM((2, 8, 128), f32),
            pltpu.VMEM((2, 8, 128), f32),
            pltpu.VMEM((ITERS, n_y, 24, 128), f32),
            pltpu.VMEM((ITERS, n_x, 24, 128), f32),
            pltpu.VMEM((16, order), bf16),
            pltpu.VMEM((16, order), bf16),
            pltpu.VMEM((16, order), bf16),
            pltpu.VMEM((8, 128), f32),
            pltpu.VMEM((8, 128), f32),
            dma((2, 8)), dma((3,)), dma((3,)),
            dma((steps, 2)), dma((steps, 2)), dma((steps, 2, 4)), dma((steps, 2, 4)),
            dma((ITERS, n_y - 1)), dma((ITERS, n_y - 1)),
            dma((ITERS, n_x - 1)), dma((ITERS, n_x - 1)),
        ],
        compiler_params=pltpu.CompilerParams(
            collective_id=0, has_side_effects=True, vmem_limit_bytes=50 * 1024 * 1024
        ),
    )(all_rows(adjoint_load), all_rows(forward_state), om, owner_index[0, 0],
      stiffness[0, 0], mass_matrix[0, 0])
    sol = sol.reshape(2, 2, slots, 4, face_len)
    sol = lax.dynamic_index_in_dim(sol, f, axis=1, keepdims=False)
    sol = jnp.swapaxes(sol, 0, 1)[None, None]
    share = DE_SUB // 2
    grad = lax.dynamic_slice_in_dim(grad.reshape(-1), f * share, share, axis=0)
    level = lax.dynamic_slice_in_dim(level[:, 0], f * slots, slots, axis=0)
    return sol, grad[None, None], level


def fits(mesh):
    return mesh.shape["freq"] == 2 and mesh.shape["sx"] > 1 and mesh.shape["sy"] > 1


def solution(mesh):
    if fits(mesh):
        run = functools.partial(fused_body, mesh.shape["sx"], mesh.shape["sy"])
    else:
        run = body
    return jax.shard_map(
        run,
        mesh=mesh,
        in_specs=(
            P("sx", "sy", None, "freq"),
            P("sx", "sy", None, "freq"),
            P(),
            P("freq"),
            P("sx", "sy", "freq", None, None, None),
            P("sx", "sy", "freq", None, None, None),
            P("sx", "sy", None, None),
        ),
        out_specs=(P("sx", "sy", "freq", None, None, None), P("sx", "sy", "freq"), P("freq")),
        check_vma=False,
    )
```

```python
import functools

import jax
import jax.numpy as jnp
from jax import lax
from jax.experimental import pallas as pl
from jax.experimental.pallas import tpu as pltpu
from jax.sharding import PartitionSpec as P

ITERS = 4
DE_SUB = 1728


LOSS_FACTOR = 0.3


def padded(cells, sides, width):
    for axis, dim in sides:
        count = lax.axis_size(axis)
        ends = count - 1
        head = lax.slice_in_dim(cells, 0, width, axis=dim)
        tail = lax.slice_in_dim(cells, cells.shape[dim] - width, cells.shape[dim], axis=dim)
        cells = jnp.concatenate(
            [
                lax.ppermute(tail, axis, [(i, (i + 1) % count) for i in range(ends)]),
                cells,
                lax.ppermute(head, axis, [((i + 1) % count, i) for i in range(ends)]),
            ],
            axis=dim,
        )
    return cells


def face_weights():
    index_x = lax.axis_index("sx")
    size_x = lax.axis_size("sx")
    index_y = lax.axis_index("sy")
    size_y = lax.axis_size("sy")
    west_weight = jnp.where(index_x > 0, 0.5, 1.0)
    east_weight = jnp.where(index_x < size_x - 1, 0.5, 1.0)
    south_weight = jnp.where(index_y > 0, 0.5, 1.0)
    north_weight = jnp.where(index_y < size_y - 1, 0.5, 1.0)
    return jnp.stack([west_weight, east_weight, south_weight, north_weight]).astype(jnp.float32)


def assemble(local_vals):
    padded_x = padded(local_vals[:, :, 0:2].astype(jnp.bfloat16), (("sx", 2),), 1).astype(
        jnp.float32
    )
    padded_y = padded(local_vals[:, :, 2:4].astype(jnp.bfloat16), (("sy", 2),), 1).astype(
        jnp.float32
    )
    west_face = padded_x[:, :, 1] + padded_x[:, :, 0]
    east_face = padded_x[:, :, 2] + padded_x[:, :, 3]
    south_face = padded_y[:, :, 1] + padded_y[:, :, 0]
    north_face = padded_y[:, :, 2] + padded_y[:, :, 3]
    return jnp.stack([west_face, east_face, south_face, north_face], axis=2)


def mix_parts(stiff_part, mass_part, omega_sq, sign_factor):
    factor = omega_sq[:, None, None]
    real_part = (
        stiff_part[:, 0] - sign_factor * LOSS_FACTOR * stiff_part[:, 1] - factor * mass_part[:, 0]
    )
    imag_part = (
        stiff_part[:, 1] + sign_factor * LOSS_FACTOR * stiff_part[:, 0] - factor * mass_part[:, 1]
    )
    return jnp.stack([real_part, imag_part], axis=1)


def apply_rows(vector, stiff_cols, mass_cols, omega_every, sign_factor):
    face_count = vector.shape[2]
    matrix_order = face_count * vector.shape[3]
    rounded = vector.astype(jnp.bfloat16)
    pieces = lax.all_gather(rounded, "freq", axis=0, tiled=True)
    count = pieces.shape[0]
    flattened = pieces.reshape(-1, matrix_order)
    stiff_part = jnp.dot(flattened, stiff_cols, preferred_element_type=jnp.float32)
    mass_part = jnp.dot(flattened, mass_cols, preferred_element_type=jnp.float32)
    local_vals = mix_parts(
        stiff_part.reshape(count, 2, face_count, -1),
        mass_part.reshape(count, 2, face_count, -1),
        omega_every,
        sign_factor,
    )
    returned = lax.all_to_all(
        local_vals.astype(jnp.bfloat16), "freq", split_axis=0, concat_axis=3, tiled=True
    ).astype(local_vals.dtype)
    return assemble(returned)


def reduce_dots(factor_pairs, weights):
    partial_value = tuple(
        (
            jnp.sum(first_vec * second_vec * weights[None, None, :, None], axis=(1, 2, 3))
            for first_vec, second_vec in factor_pairs
        )
    )
    summed = lax.psum(partial_value, ("sx", "sy"))
    return summed


def per_freq(values):
    return values[:, None, None, None]


def face_columns(matrix, matrix_order, face_count):
    grouped = matrix.reshape(matrix_order, -1, face_count)
    return jnp.swapaxes(grouped, 1, 2).reshape(matrix_order, -1)


def body(stiffness, mass_matrix, omega_table, assignment, adjoint_load, forward_state, owner_index):
    n_freq = lax.axis_size("freq")
    slot_count = adjoint_load.shape[2]
    face_count = adjoint_load.shape[4]
    face_len = adjoint_load.shape[5]
    matrix_order = face_count * face_len
    stiff_cols = face_columns(stiffness[0, 0], matrix_order, face_count)
    mass_cols = face_columns(mass_matrix[0, 0], matrix_order, face_count)
    matches = assignment[:, None] == jnp.arange(omega_table.shape[0], dtype=jnp.int32)[None, :]
    slot_omega = jnp.sum(jnp.where(matches, omega_table[None, :], 0.0), axis=1)
    weights = face_weights()
    load_rows = adjoint_load[0, 0]
    omega_every = lax.all_gather(slot_omega, "freq", axis=0, tiled=True)

    def operate(vector, sign_factor):
        return apply_rows(vector, stiff_cols, mass_cols, omega_every, sign_factor)

    residual = load_rows
    solution = jnp.zeros_like(load_rows)
    normal_res = operate(residual, -1.0)
    direction = normal_res
    image_vec = operate(normal_res, 1.0)
    gamma_now, delta_now = reduce_dots(((normal_res, normal_res), (image_vec, image_vec)), weights)
    for iteration in range(ITERS):
        step_size = gamma_now / delta_now
        solution = solution + per_freq(step_size) * direction
        if iteration + 1 < ITERS:
            residual = residual - per_freq(step_size) * image_vec
            normal_res = operate(residual, -1.0)
            fresh = operate(normal_res, 1.0)
            gamma_next, fresh_norm, fresh_cross = reduce_dots(
                ((normal_res, normal_res), (fresh, fresh), (fresh, image_vec)), weights
            )
            beta_ratio = gamma_next / gamma_now
            direction = normal_res + per_freq(beta_ratio) * direction
            image_vec = fresh + per_freq(beta_ratio) * image_vec
            delta_now = (
                fresh_norm + 2.0 * beta_ratio * fresh_cross + beta_ratio * beta_ratio * delta_now
            )
            gamma_now = gamma_next
    cell_count = float(lax.axis_size("sx") * lax.axis_size("sy") * 2 * matrix_order)
    residual_level = jnp.log(gamma_now / cell_count)
    state_vec = forward_state[0, 0].astype(jnp.float32)
    lambda_real = solution[:, 0]
    lambda_imag = solution[:, 1]
    state_real = state_vec[:, 0]
    state_imag = state_vec[:, 1]
    product_term = (
        lambda_real * state_real
        - lambda_imag * state_imag
        - LOSS_FACTOR * (lambda_real * state_imag + lambda_imag * state_real)
    )
    dof_total = jnp.sum(product_term, axis=0)
    partial_grad = jax.ops.segment_sum(
        dof_total.reshape(-1), owner_index[0, 0].reshape(-1), num_segments=DE_SUB
    )
    grad_factor = (DE_SUB / (slot_count * n_freq * matrix_order)) ** 0.5
    gradient = lax.psum_scatter(
        -grad_factor * partial_grad, "freq", scatter_dimension=0, tiled=True
    )
    return (solution[None, None], gradient[None, None], residual_level)


MESH = pl.DeviceIdType.MESH


def fused_kernel(
    sizes, load, state_in, table, slot_of, own, stiff, mass, out_sol, out_grad, out_lvl,
    stage, mats, acc, vbuf, ysend, yrecv, frecv, state, dacc, scal, hist,
    red_y, red_x, ld, ldr, st, stb, om, omr, omw,
    mat_sem, pro_send, pro_recv, vs_sem, vr_sem, fs_sem, fr_sem,
    ys_sem, yr_sem, xs_sem, xr_sem,
):
    n_x, n_y, face_len, cells, grad_factor = sizes
    seg = face_len // 2
    half = 2 * seg
    blocks = seg // 128
    f = lax.axis_index("freq")
    ix = lax.axis_index("sx")
    iy = lax.axis_index("sy")
    other = 1 - f
    N, PD, Q, W, FR, SOL = range(6)

    def mat_copy(m, r):
        src = stiff if m == 0 else mass
        off = (2 * (r // 4) + r % 2) * face_len + ((f + r // 2) % 2) * seg
        return pltpu.make_async_copy(
            src.at[pl.ds(pl.multiple_of(off, 128), seg)], stage.at[m, r], mat_sem.at[m, r]
        )

    for r in range(8):
        for m in range(2):
            mat_copy(m, r).start()

    state[...] = jnp.zeros_like(state)
    dacc[...] = jnp.zeros_like(dacc)
    hist[...] = jnp.zeros_like(hist)
    scal[0] = jnp.full((8, 128), -1.0, jnp.float32)
    scal[1] = jnp.zeros((8, 128), jnp.float32)

    has = (ix > 0, ix < n_x - 1, iy > 0, iy < n_y - 1)
    peer = ({"sx": ix - 1}, {"sx": ix + 1}, {"sy": iy - 1}, {"sy": iy + 1})
    for d in range(4):
        @pl.when(jnp.logical_not(has[d]))
        def _(d=d):
            frecv[:, :, d] = jnp.zeros_like(frecv[:, :, d])

    slots = slot_of.shape[0]
    ld[...] = jnp.zeros_like(ld)
    st[...] = jnp.zeros_like(st)
    line = lax.broadcasted_iota(jnp.int32, (8, 128), 0)
    spots = jnp.zeros((8, 128), jnp.float32)
    for s in range(slots):
        value = jnp.float32(0.0)
        for j in range(table.shape[0]):
            value = value + jnp.where(slot_of[s] == j, table[j], 0.0)
        spots = jnp.where(line == f * slots + s, value, spots)
        for c in range(2):
            for src, dst in ((load, ld), (state_in, st)):
                tile = src[s, c].astype(jnp.float32)
                for face in range(4):
                    at = pl.ds(8 * c + f * slots + s, 1)
                    dst[at, face * face_len : (face + 1) * face_len] = tile[face : face + 1]
    om[...] = spots

    barrier = pltpu.get_barrier_semaphore()
    for side in range(2):
        where = {"freq": (f + side) % 2}
        for d in range(1, n_x):
            pl.semaphore_signal(
                barrier, inc=1, device_id={"sx": (ix + d) % n_x, **where}, device_id_type=MESH
            )
        for d in range(1, n_y):
            pl.semaphore_signal(
                barrier, inc=1, device_id={"sy": (iy + d) % n_y, **where}, device_id_type=MESH
            )
    pl.semaphore_signal(barrier, inc=1, device_id={"freq": other}, device_id_type=MESH)
    pl.semaphore_wait(barrier, 2 * (n_x + n_y - 2) + 1)

    def to_partner(src, dst, ssem, rsem):
        return pltpu.make_async_remote_copy(
            src_ref=src, dst_ref=dst, send_sem=ssem, recv_sem=rsem,
            device_id={"freq": other}, device_id_type=MESH,
        )

    prologue = [
        to_partner(ld, ldr, pro_send.at[0], pro_recv.at[0]),
        to_partner(om, omr, pro_send.at[1], pro_recv.at[1]),
        to_partner(st, stb, pro_send.at[2], pro_recv.at[2]),
    ]
    for copy in prologue:
        copy.start()

    row = lax.broadcasted_iota(jnp.int32, (256, 256), 0)
    col = lax.broadcasted_iota(jnp.int32, (256, 256), 1)
    spread = [
        jnp.where(row == 4 * (col % 64) + ((col // 64) ^ flip), 1.0, 0.0).astype(jnp.bfloat16)
        for flip in range(2)
    ]
    first = lax.broadcasted_iota(jnp.int32, (seg, 128), 1) < 64

    def place(r, carry):
        rows = pl.ds(pl.multiple_of(r * seg, 128), seg)
        for m in range(2):
            mat_copy(m, r).wait()
            for b in range(blocks):
                lower, upper = (
                    jnp.dot(
                        stage[m, r, :, b * 512 + i * 256 : b * 512 + (i + 1) * 256], spread[i],
                        preferred_element_type=jnp.float32,
                    )
                    for i in range(2)
                )
                for h in range(2):
                    a, z = lower[:, h * 128 : (h + 1) * 128], upper[:, h * 128 : (h + 1) * 128]
                    lo = h * half + b * 128
                    even, odd = jnp.where(first, a, z), jnp.where(first, z, a)
                    mats[m, rows, lo : lo + 128] = even.astype(jnp.bfloat16)
                    mats[m, rows, lo + seg : lo + seg + 128] = odd.astype(jnp.bfloat16)
        return carry

    lax.fori_loop(0, 8, place, 0)

    for copy in prologue[:2]:
        copy.wait()
    omw[...] = om[...] + omr[...]
    def pieces(h):
        for j in range(4):
            side, face = j // 2, 2 * h + j % 2
            here = ((f + side) % 2) * seg
            at = pl.ds(pl.multiple_of(face * face_len + here, 128), seg)
            yield face, here, at, slice(j * seg, (j + 1) * seg)

    for h in range(2):
        for _, _, at, cut in pieces(h):
            vbuf[h, 0:16, cut] = (ld[:, at] + ldr[:, at]).astype(jnp.bfloat16)
        vbuf[h, 16:32] = jnp.zeros((16, 2 * half), jnp.bfloat16)

    def y_copy(t, h):
        return to_partner(ysend.at[t, h], yrecv.at[t, h], vs_sem.at[t, h], vr_sem.at[t, h])

    def face_copy(t, side, d, land):
        where = {"freq": (f + side) % 2} if side else {}
        return pltpu.make_async_remote_copy(
            src_ref=ysend.at[t, d // 2, :, pl.ds((d % 2) * seg, seg)],
            dst_ref=frecv.at[t, side, land],
            send_sem=fs_sem.at[t, side, d], recv_sem=fr_sem.at[t, side, land],
            device_id={**peer[d], **where}, device_id_type=MESH,
        )

    def send_values(t, h):
        for d in (2 * h, 2 * h + 1):
            @pl.when(has[d])
            def _(d=d):
                for side in range(2):
                    face_copy(t, side, d, d ^ 1).start()
        y_copy(t, h).start()

    def take_values(t, h):
        for d in (2 * h, 2 * h + 1):
            @pl.when(has[d])
            def _(d=d):
                for side in range(2):
                    face_copy(t, side, d, d).wait()
        y_copy(t, h).wait()
        got = [frecv[t, j // 2, 2 * h + j % 2] for j in range(4)]
        local = jnp.concatenate([ysend[t, h], yrecv[t, h]], axis=1)
        return local + jnp.concatenate(got, axis=1)

    def both(x):
        return jnp.concatenate([x, x], axis=0)[:, :1]

    def lanes(x):
        x = x[0:8] + x[8:16]
        total = x[:, 0:128]
        for b in range(1, blocks):
            total = total + x[:, b * 128 : (b + 1) * 128]
        return total

    def finish_adjoint(t, h):
        u = take_values(t, h)
        alpha, beta = both(scal[0]), both(scal[1])
        w = u + beta * state[W, h]
        n = state[N, h]
        p = n + beta * state[PD, h]
        state[Q, h] = state[FR, h] + beta * state[Q, h]
        state[PD, h] = p
        state[W, h] = w
        state[SOL, h] = state[SOL, h] + alpha * p
        n = n - alpha * w
        state[N, h] = n
        return n

    def finish_image(t, h):
        fresh = take_values(t, h)
        state[FR, h] = fresh
        n, q = state[N, h], state[Q, h]
        for face, _, _, cut in pieces(h):
            weight = jnp.where(has[face], 0.5, 1.0).astype(jnp.float32)
            for i, (a, b) in enumerate(((n, n), (fresh, fresh), (fresh, q))):
                part = weight * lanes(a[:, cut] * b[:, cut])
                dacc[8 * i : 8 * i + 8] = dacc[8 * i : 8 * i + 8] + part
        return fresh

    def pass_on(h, value):
        high = value.astype(jnp.bfloat16)
        vbuf[h, 0:16] = high
        vbuf[h, 16:32] = (value - high.astype(jnp.float32)).astype(jnp.bfloat16)

    def ring_copies(it, buf, axis, me, count, ssem, rsem):
        return [
            pltpu.make_async_remote_copy(
                src_ref=buf.at[it, me], dst_ref=buf.at[it, me],
                send_sem=ssem.at[it, d - 1], recv_sem=rsem.at[it, d - 1],
                device_id={axis: (me + d) % count}, device_id_type=MESH,
            )
            for d in range(1, count)
        ]

    def over_y(it):
        return ring_copies(it, red_y, "sy", iy, n_y, ys_sem, yr_sem)

    def over_x(it):
        return ring_copies(it, red_x, "sx", ix, n_x, xs_sem, xr_sem)

    def reduce_start(it):
        red_y[it, iy] = dacc[...]
        dacc[...] = jnp.zeros_like(dacc)
        for copy in over_y(it):
            copy.start()

    def reduce_mid(it):
        for copy in over_y(it):
            copy.wait()
        total = red_y[it, 0]
        for j in range(1, n_y):
            total = total + red_y[it, j]
        red_x[it, ix] = total
        for copy in over_x(it):
            copy.start()

    def reduce_end(it):
        for copy in over_x(it):
            copy.wait()
        total = red_x[it, 0]
        for j in range(1, n_x):
            total = total + red_x[it, j]
        total = jnp.broadcast_to(jnp.sum(total, axis=1, keepdims=True), (24, 128))
        gamma, norm, cross = total[0:8], total[8:16], total[16:24]
        beta = jnp.where(it > 0, gamma / hist[0], 0.0)
        delta = norm + 2.0 * beta * cross + beta * beta * hist[1]
        hist[0] = gamma
        hist[1] = delta
        scal[0] = gamma / delta
        scal[1] = beta

    def products(m, rows, h):
        out = jnp.dot(
            vbuf[rows],
            mats[m, rows * 2 * half : (rows + 1) * 2 * half, h * half : (h + 1) * half],
            preferred_element_type=jnp.float32,
        )
        return out[0:16] + out[16:32]

    def apply(t, carry):
        it = t // 2
        adjoint_step = t % 2 == 0
        reducing = jnp.logical_and(adjoint_step, t > 0)
        sign = (2 * (t % 2) - 1).astype(jnp.float32) * LOSS_FACTOR
        for h in range(2):
            for m in range(2):
                acc[m, h] = products(m, 0, h)

        @pl.when(reducing)
        def _():
            pass_on(1, finish_image(t - 1, 1))
            reduce_start(it - 1)

        @pl.when(jnp.logical_not(adjoint_step))
        def _():
            pass_on(1, finish_adjoint(t - 1, 1))

        omega = both(omw[...])[0:8]
        for h in range(2):
            stiff_part, mass_part = (acc[m, h] + products(m, 1, h) for m in range(2))
            real = stiff_part[0:8] - sign * stiff_part[8:16] - omega * mass_part[0:8]
            imag = stiff_part[8:16] + sign * stiff_part[0:8] - omega * mass_part[8:16]
            for c, values in enumerate((real, imag)):
                ysend[t, h, 8 * c : 8 * c + 8, 0:seg] = values[:, 0:seg]
                for b in range(blocks):
                    lo = seg + b * 128
                    turned = pltpu.roll(values[:, lo : lo + 128], 64, 1)
                    ysend[t, h, 8 * c : 8 * c + 8, lo : lo + 128] = turned
            send_values(t, h)
            if h == 0:
                @pl.when(reducing)
                def _():
                    reduce_mid(it - 1)

        @pl.when(reducing)
        def _():
            reduce_end(it - 1)

        @pl.when(adjoint_step)
        def _():
            pass_on(0, finish_adjoint(t, 0))

        @pl.when(jnp.logical_not(adjoint_step))
        def _():
            pass_on(0, finish_image(t, 0))

        return carry

    lax.fori_loop(0, 2 * ITERS, apply, 0)

    finish_image(2 * ITERS - 1, 1)
    reduce_start(ITERS - 1)
    reduce_mid(ITERS - 1)
    reduce_end(ITERS - 1)
    out_lvl[...] = jnp.log(hist[0] / cells)
    alpha, beta = both(scal[0]), both(scal[1])
    for h in range(2):
        state[SOL, h] = state[SOL, h] + alpha * (state[N, h] + beta * state[PD, h])

    prologue[2].wait()
    bins = jnp.zeros((16, 128), jnp.float32)
    for h in range(2):
        for face, here, at, cut in pieces(h):
            lam = state[SOL, h, :, cut]
            out_sol[:, at] = lam
            u = st[:, at] + stb[:, at]
            lr, li, ur, ui = lam[0:8], lam[8:16], u[0:8], u[8:16]
            term = lr * ur - li * ui - LOSS_FACTOR * (lr * ui + li * ur)
            dof = jnp.sum(term, axis=0, keepdims=True)
            owner = own[face : face + 1, pl.ds(pl.multiple_of(here, 128), seg)]
            high = lax.broadcasted_iota(jnp.int32, (16, seg), 0) == owner // 128
            low = lax.broadcasted_iota(jnp.int32, (128, seg), 0) == owner % 128
            low = jnp.where(low, 1.0, 0.0).astype(jnp.bfloat16)
            rest = jnp.where(high, dof, 0.0)
            for _ in range(3):
                piece = rest.astype(jnp.bfloat16)
                bins = bins + lax.dot_general(
                    piece, low, (((1,), (1,)), ((), ())), preferred_element_type=jnp.float32
                )
                rest = rest - piece.astype(jnp.float32)
    out_grad[...] = -grad_factor * bins


def fused_body(n_x, n_y, stiffness, mass_matrix, omega_table, assignment, adjoint_load, forward_state, owner_index):
    f = lax.axis_index("freq")
    slots = adjoint_load.shape[2]
    face_len = adjoint_load.shape[5]
    order = 4 * face_len
    seg = face_len // 2
    f32, bf16 = jnp.float32, jnp.bfloat16
    steps = 2 * ITERS
    half = 2 * seg
    dma = pltpu.SemaphoreType.DMA
    vmem = pl.BlockSpec(memory_space=pltpu.VMEM)
    hbm = pl.BlockSpec(memory_space=pl.ANY)
    smem = pl.BlockSpec(memory_space=pltpu.SMEM)
    grad_factor = (DE_SUB / (2 * slots * order)) ** 0.5
    sizes = (n_x, n_y, face_len, float(n_x * n_y * 2 * order), grad_factor)
    sol, grad, level = pl.pallas_call(
        functools.partial(fused_kernel, sizes),
        out_shape=(
            jax.ShapeDtypeStruct((16, order), f32),
            jax.ShapeDtypeStruct((16, 128), f32),
            jax.ShapeDtypeStruct((8, 128), f32),
        ),
        in_specs=[vmem, vmem, smem, smem, vmem, hbm, hbm],
        out_specs=(vmem, vmem, vmem),
        scratch_shapes=[
            pltpu.VMEM((2, 8, seg, half * 2), bf16),
            pltpu.VMEM((2, order, half * 2), bf16),
            pltpu.VMEM((2, 2, 16, half), f32),
            pltpu.VMEM((2, 32, 2 * half), bf16),
            pltpu.VMEM((steps, 2, 16, half), f32),
            pltpu.VMEM((steps, 2, 16, half), f32),
            pltpu.VMEM((steps, 2, 4, 16, seg), f32),
            pltpu.VMEM((6, 2, 16, 2 * half), f32),
            pltpu.VMEM((24, 128), f32),
            pltpu.VMEM((2, 8, 128), f32),
            pltpu.VMEM((2, 8, 128), f32),
            pltpu.VMEM((ITERS, n_y, 24, 128), f32),
            pltpu.VMEM((ITERS, n_x, 24, 128), f32),
            pltpu.VMEM((16, order), f32),
            pltpu.VMEM((16, order), f32),
            pltpu.VMEM((16, order), f32),
            pltpu.VMEM((16, order), f32),
            pltpu.VMEM((8, 128), f32),
            pltpu.VMEM((8, 128), f32),
            pltpu.VMEM((8, 128), f32),
            dma((2, 8)), dma((3,)), dma((3,)),
            dma((steps, 2)), dma((steps, 2)), dma((steps, 2, 4)), dma((steps, 2, 4)),
            dma((ITERS, n_y - 1)), dma((ITERS, n_y - 1)),
            dma((ITERS, n_x - 1)), dma((ITERS, n_x - 1)),
        ],
        compiler_params=pltpu.CompilerParams(
            collective_id=0, has_side_effects=True, vmem_limit_bytes=50 * 1024 * 1024
        ),
    )(adjoint_load[0, 0], forward_state[0, 0], omega_table, assignment, owner_index[0, 0],
      stiffness[0, 0], mass_matrix[0, 0])
    sol = sol.reshape(2, 2, slots, 4, face_len)
    sol = lax.dynamic_index_in_dim(sol, f, axis=1, keepdims=False)
    sol = jnp.swapaxes(sol, 0, 1)[None, None]
    share = DE_SUB // 2
    grad = lax.dynamic_slice_in_dim(grad.reshape(-1), f * share, share, axis=0)
    level = lax.dynamic_slice_in_dim(level[:, 0], f * slots, slots, axis=0)
    return sol, grad[None, None], level


def fits(mesh):
    return mesh.shape["freq"] == 2 and mesh.shape["sx"] > 1 and mesh.shape["sy"] > 1


def solution(mesh):
    if fits(mesh):
        run = functools.partial(fused_body, mesh.shape["sx"], mesh.shape["sy"])
    else:
        run = body
    return jax.shard_map(
        run,
        mesh=mesh,
        in_specs=(
            P("sx", "sy", None, "freq"),
            P("sx", "sy", None, "freq"),
            P(),
            P("freq"),
            P("sx", "sy", "freq", None, None, None),
            P("sx", "sy", "freq", None, None, None),
            P("sx", "sy", None, None),
        ),
        out_specs=(P("sx", "sy", "freq", None, None, None), P("sx", "sy", "freq"), P("freq")),
        check_vma=False,
    )
```
